128 devices in a mesh: node: 16 (over x, z), dev: 8 (over y, core).
Axes of the slice: x: 4, y: 4, z: 4, core: 2. Of those that a mesh axis runs over, the one named last changes fastest.
Arguments:
- old_state: float32 [16384, 5, 512], P(('node', 'dev')), as said below
- old_tile_pos: int32 [16384], P(('node', 'dev')), may hold values from 0 to 16383, as said below
Outputs:
- stepped_state: float32 [5, 256, 256, 128], P(None, 'node', 'dev')
The draws below stay inside these ranges and needn't reach their ends.
Inputs may be any that keep to these rules, and one draw needn't show every extreme that they name: Cells of old_state have density 0.5 to 2, velocity components -1 to 1 and pressure 0.5 to 2. A permutation. The tile in old slot s of device d goes to device old_tile_pos[s] // 128, which is d itself, a device within 4 of d in the order of node+dev (node slowest, no wrap), or the device (d + 64) mod 128. At most 8 tiles go from one device to another, and as many come back; every device exchanges exactly 8 tiles with the device 128 // 2 away, and in every draw some device exchanges exactly 8 tiles with each of the 8 devices within reach.
All inputs are finite; a program needn't handle non-finite values.
Results may differ from the reference program's by a relative error of at most 0.0003.
Values sent between devices are 32-bit elements; how exact they have to be, the bound alone decides.
No kernel may reach another device: no remote copies, remote signals or barrier semaphores. Data moves between devices by JAX's collectives and lax.ppermute only.
A program may use at most 128 MiB of HBM per device.

```python
import math
import jax
import jax.numpy as jnp
from jax import lax

CX = 16
CY = 32
CZ = 128
FIELDS = 5
TILE = 8
REACH = 4
MOVE = 8
TILE_CELLS = 512
TILES_DEV = 128
NTILES = 16384
NX = 256
NY = 256
NZ = 128
N_NODE = 16
N_DEV = 8
DEVICES = 128


def draw_old_state(key, part):
    key = jax.random.fold_in(key, 11)
    subkeys = jax.random.split(key, 3)
    cell_shape = (NTILES, TILE_CELLS)
    density = jnp.exp(jax.random.uniform(subkeys[0], cell_shape, jnp.float32, math.log(0.5), math.log(2.0)))
    velocity = jnp.clip(0.45 * jax.random.normal(subkeys[1], (3,) + cell_shape, jnp.float32), -1.0, 1.0)
    pressure = jax.random.uniform(subkeys[2], cell_shape, jnp.float32, 0.5, 2.0)
    momenta = density[None] * velocity
    energy = pressure / 0.4 + 0.5 * density * jnp.sum(velocity * velocity, axis=0)
    return jnp.stack([density, momenta[0], momenta[1], momenta[2], energy], axis=1).astype(jnp.float32)


def draw_old_tile_pos(key, part):
    key = jax.random.fold_in(key, 23)
    key_orders, key_pairs, key_focus = jax.random.split(key, 3)
    device_ids = jnp.arange(DEVICES, dtype=jnp.int32)
    orders = jax.vmap(lambda subkey: jax.random.permutation(subkey, TILES_DEV))(jax.random.split(key_orders, DEVICES)).astype(jnp.int32)
    steps_ahead = jnp.arange(1, REACH + 1, dtype=jnp.int32)
    pair_count = jax.random.randint(key_pairs, (DEVICES, REACH), 0, MOVE + 1, dtype=jnp.int32)
    focused = jax.random.randint(key_focus, (), REACH, DEVICES - REACH, dtype=jnp.int32)
    forced = (device_ids[:, None] == focused) | (device_ids[:, None] + steps_ahead[None, :] == focused)
    pair_count = jnp.where(forced, MOVE, pair_count)
    pair_count = jnp.where(device_ids[:, None] + steps_ahead[None, :] < DEVICES, pair_count, 0)
    behind_source = device_ids[:, None] - steps_ahead[None, :]
    behind_count = pair_count[jnp.clip(behind_source, 0, DEVICES - 1), jnp.arange(REACH)[None, :]]
    behind_count = jnp.where(behind_source >= 0, behind_count, 0)
    far_partner = (device_ids + DEVICES // 2) % DEVICES
    far_count = jnp.full((DEVICES, 1), MOVE, jnp.int32)
    counts = jnp.concatenate([pair_count, behind_count, far_count], axis=1)
    partners = jnp.concatenate([device_ids[:, None] + steps_ahead[None, :], behind_source, far_partner[:, None]], axis=1)
    starts = jnp.cumsum(counts, axis=1) - counts
    positions = jnp.arange(TILES_DEV, dtype=jnp.int32)
    inside = (positions[None, :, None] >= starts[:, None, :]) & (positions[None, :, None] < (starts + counts)[:, None, :])
    inside_int = inside.astype(jnp.int32)
    has_partner = jnp.sum(inside_int, axis=2) > 0
    block_index = jnp.sum(inside_int * jnp.arange(2 * REACH + 1, dtype=jnp.int32)[None, None, :], axis=2)
    rank = positions[None, :] - jnp.take_along_axis(starts, block_index, axis=1)
    partner = jnp.clip(jnp.take_along_axis(partners, block_index, axis=1), 0, DEVICES - 1)
    partner_block = jnp.where(block_index < REACH, block_index + REACH, jnp.where(block_index < 2 * REACH, block_index - REACH, block_index))
    mirror = jnp.clip(starts[partner, partner_block] + rank, 0, TILES_DEV - 1)
    target = jnp.where(has_partner, partner * TILES_DEV + orders[partner, mirror], device_ids[:, None] * TILES_DEV + orders)
    result = jnp.zeros((DEVICES, TILES_DEV), jnp.int32).at[device_ids[:, None], orders].set(target)
    return result.reshape(-1)


def setup_inputs(seed: int = 0) -> dict:
    splits = jax.random.split(jax.random.key(seed), 3)
    old_state = draw_old_state(jax.random.fold_in(splits[2], 71), 0)
    old_tile_pos = draw_old_tile_pos(jax.random.fold_in(splits[2], 71), 0)
    return dict(old_state=old_state, old_tile_pos=old_tile_pos)


gamma_gas = 1.4
time_ratio = 0.1

def cut_range(values, first_cell, cell_count, direction):
    return lax.slice_in_dim(values, first_cell, first_cell + cell_count, axis=direction)

def median_zero(first_value, second_value):
    return jnp.maximum(jnp.minimum(first_value, 0.0), jnp.minimum(jnp.maximum(first_value, 0.0), second_value))

def primitives(conserved):
    density = conserved[0]
    velocity = conserved[1:4] / density
    pressure = (gamma_gas - 1.0) * (conserved[4] - 0.5 * density * lax.optimization_barrier(jnp.sum(velocity * velocity, axis=0)))
    return jnp.concatenate([density[None], velocity, pressure[None]], axis=0)

def state_terms(primitive, direction):
    density = primitive[0]
    velocity = primitive[1:4]
    pressure = primitive[4]
    normal = primitive[direction]
    energy = pressure / (gamma_gas - 1.0) + 0.5 * density * lax.optimization_barrier(jnp.sum(velocity * velocity, axis=0))
    momenta = density * velocity
    amounts = jnp.concatenate([density[None], momenta, energy[None]], axis=0)
    flux_rows = [momenta[direction - 1]]
    for column in range(3):
        if column == direction - 1:
            flux_rows.append(momenta[column] * normal + pressure)
        else:
            flux_rows.append(momenta[column] * normal)
    flux_rows.append(normal * (energy + pressure))
    sound_speed = jnp.sqrt(gamma_gas * pressure / density)
    return (amounts, jnp.stack(flux_rows, axis=0), normal, sound_speed)

def hlle_flux(state_left, state_right, direction):
    amount_left, flux_left, speed_left, sound_left = state_terms(state_left, direction)
    amount_right, flux_right, speed_right, sound_right = state_terms(state_right, direction)
    slowest = jnp.minimum(jnp.minimum(speed_left - sound_left, speed_right - sound_right), 0.0)
    fastest = jnp.maximum(jnp.maximum(speed_left + sound_left, speed_right + sound_right), 0.0)
    numerator = fastest * flux_left - slowest * flux_right + slowest * fastest * (amount_right - amount_left)
    return numerator / (fastest - slowest)

def face_flux(primitive, direction):
    cell_count = primitive.shape[direction] - 6
    cell_here = cut_range(primitive, 1, cell_count + 3, direction)
    cell_next = cut_range(primitive, 2, cell_count + 3, direction)
    cell_prev = cut_range(primitive, 0, cell_count + 3, direction)
    cell_far = cut_range(primitive, 3, cell_count + 3, direction)
    interface = 7.0 / 12.0 * (cell_here + cell_next) - 1.0 / 12.0 * (cell_prev + cell_far)
    interface = jnp.clip(interface, jnp.minimum(cell_here, cell_next), jnp.maximum(cell_here, cell_next))
    centre = cut_range(primitive, 2, cell_count + 2, direction)
    diff_low = cut_range(interface, 0, cell_count + 2, direction) - centre
    diff_high = cut_range(interface, 1, cell_count + 2, direction) - centre
    edge_low = centre + median_zero(diff_low, -2.0 * diff_high)
    edge_high = centre + median_zero(diff_high, -2.0 * diff_low)
    state_left = cut_range(edge_high, 0, cell_count + 1, direction)
    state_right = cut_range(edge_low, 1, cell_count + 1, direction)
    return hlle_flux(state_left, state_right, direction)

def update(centre, line_data):
    change = jnp.zeros_like(centre)
    for direction in range(1, 4):
        flux_terms = face_flux(line_data[direction - 1], direction)
        length_cells = centre.shape[direction]
        change = change + cut_range(flux_terms, 1, length_cells, direction) - cut_range(flux_terms, 0, length_cells, direction)
    return centre - time_ratio * change

def advance(slab_block):
    centre = slab_block[:, 3:-3, 3:-3, 3:-3]
    primitive = primitives(slab_block)
    line_data = (primitive[:, :, 3:-3, 3:-3], primitive[:, 3:-3, :, 3:-3], primitive[:, 3:-3, 3:-3, :])
    return update(centre, line_data)

def reference(old_state, old_tile_pos):
    new_tiles = jnp.zeros_like(old_state).at[old_tile_pos].set(old_state)
    grid_cells = new_tiles.reshape(N_NODE, N_DEV, CX // TILE, CY // TILE, CZ // TILE, FIELDS, TILE, TILE, TILE)
    grid_cells = grid_cells.transpose(5, 0, 2, 6, 1, 3, 7, 4, 8).reshape(FIELDS, NX, NY, NZ)
    padded = jnp.pad(grid_cells, ((0, 0), (3, 3), (3, 3), (3, 3)), mode='wrap')

    def one_block(block_index):
        first_cell = (block_index * CX).astype(jnp.int32)
        slab_block = lax.dynamic_slice_in_dim(padded, first_cell, CX + 6, axis=1)
        return advance(slab_block)
    stepped = lax.map(one_block, jnp.arange(N_NODE, dtype=jnp.int32))
    return stepped.transpose(1, 0, 2, 3, 4).reshape(FIELDS, NX, NY, NZ)
```

```python
import jax
import jax.numpy as jnp
from jax import lax
from jax.experimental import pallas as pl
from jax.experimental.pallas import tpu as pltpu
from jax.sharding import PartitionSpec as P

CX = 16
CY = 32
CZ = 128
FIELDS = 5
TILE = 8
MOVE = 8
TILES = 128
CELLS = 512
PARTS = CELLS // CZ
PLANES = FIELDS * PARTS + 1
ROWS = FIELDS * CX * CY
VMEM_LIMIT = 48 * 1024 * 1024

ROW_HALF = 64
ROW_FAR = 72
ROW_RELAY = 80
ROW_END = 112

AXES = ("node", "dev")


def iota(shape, dim):
    return lax.broadcasted_iota(jnp.int32, shape, dim)


def split3(value):
    high = value.astype(jnp.bfloat16)
    rest = value - high.astype(jnp.float32)
    mid = rest.astype(jnp.bfloat16)
    low = (rest - mid.astype(jnp.float32)).astype(jnp.bfloat16)
    return high, mid, low


def pick(choice, values):
    total = None
    for part in reversed(split3(values)):
        term = jnp.dot(choice, part, preferred_element_type=jnp.float32)
        total = term if total is None else total + term
    return total


def pack_kernel(me_ref, pos_ref, old_ref, near_ref, half_ref, far_ref, relay_ref):
    me = me_ref[0]
    node, dev = me // 8, me % 8
    pos = pos_ref[...]
    square = (TILES, TILES)
    by_lane = jnp.broadcast_to(pos // TILES, square)
    by_row = by_lane.T
    earlier = (by_lane == by_row) & (iota(square, 0) < iota(square, 1))
    rank = jnp.sum(earlier.astype(jnp.int32), axis=0, keepdims=True)
    owner = pos // TILES
    local = pos % TILES
    owner_node, owner_dev = owner // 8, owner % 8
    inside = jnp.where(jnp.abs(owner_dev - dev) == 4, ROW_HALF, owner_dev * MOVE)
    outside = jnp.where(owner_node == node ^ 8, ROW_FAR, ROW_RELAY + (owner_dev % 4) * MOVE)
    base = jnp.where(owner_node == node, inside, outside)
    target = jnp.where(owner == me, -1, base + rank)
    shape = (ROW_END, TILES)
    chosen = iota(shape, 0) == jnp.broadcast_to(target, shape)
    code = jnp.sum(
        jnp.where(chosen, jnp.broadcast_to(local + 1, shape), 0).astype(jnp.float32), axis=1, keepdims=True
    )
    code = jnp.broadcast_to(code, shape)
    choice = chosen.astype(jnp.float32).astype(jnp.bfloat16)

    def put(plane, value):
        for block in range(8):
            near_ref[block, plane] = value[block * MOVE : (block + 1) * MOVE]
        half_ref[plane] = value[ROW_HALF:ROW_FAR]
        far_ref[plane] = value[ROW_FAR:ROW_RELAY]
        for block in range(4):
            first = ROW_RELAY + block * MOVE
            relay_ref[block, plane] = value[first : first + MOVE]

    put(PLANES - 1, code)
    for field in range(FIELDS):
        rows = pick(choice, old_ref[field])
        for part in range(PARTS):
            put(field * PARTS + part, rows[:, part * CZ : (part + 1) * CZ])


def pack(me, pos, old):
    buffer = jax.ShapeDtypeStruct((PLANES, MOVE, CZ), jnp.float32)
    near = jax.ShapeDtypeStruct((8,) + buffer.shape, jnp.float32)
    relay = jax.ShapeDtypeStruct((4,) + buffer.shape, jnp.float32)
    vmem = pl.BlockSpec(memory_space=pltpu.VMEM)
    return pl.pallas_call(
        pack_kernel,
        out_shape=(near, buffer, buffer, relay),
        in_specs=[pl.BlockSpec(memory_space=pltpu.SMEM), vmem, vmem],
        out_specs=(vmem, vmem, vmem, vmem),
        compiler_params=pltpu.CompilerParams(vmem_limit_bytes=VMEM_LIMIT),
        name="pack",
    )(me, pos, old)


def grains(first, second, half_low, row_pick, lane_picks):
    first = pltpu.roll(first, 0, 1, stride=TILE, stride_axis=0)
    second = pltpu.roll(second, 64, 1, stride=TILE, stride_axis=0)
    result = []
    for half in range(2):
        mixed = jnp.where(half_low, first, second) if half == 0 else jnp.where(half_low, second, first)
        mixed = jnp.take_along_axis(mixed, row_pick, axis=0)
        result.append(jnp.take_along_axis(mixed, lane_picks[half], axis=1))
    return result


def unpack_kernel(
    me_ref, pos_ref, old_ref, near_ref, half_ref, far_ref,
    state_ref, prim_ref, x_low_ref, x_high_ref, y_low_ref, y_high_ref, tiles_ref,
):
    me = me_ref[0]
    pos = pos_ref[...]
    square = (TILES, TILES)
    kept = jnp.where(pos // TILES == me, pos % TILES, -1)
    kept_choice = jnp.broadcast_to(kept, square) == iota(square, 0)

    def arrived(plane):
        return jnp.concatenate(
            [near_ref[block, plane] for block in range(8)] + [half_ref[plane], far_ref[plane]], axis=0
        )

    code = jnp.concatenate([arrived(PLANES - 1), jnp.zeros((48, CZ), jnp.float32)], axis=0)
    code = code.T.astype(jnp.int32)
    new_choice = code == iota(square, 0) + 1
    choice = jnp.concatenate([kept_choice, new_choice], axis=1).astype(jnp.float32).astype(jnp.bfloat16)
    blank = jnp.zeros((48, CELLS), jnp.float32)
    for field in range(FIELDS):
        moved = jnp.concatenate([arrived(field * PARTS + part) for part in range(PARTS)], axis=1)
        tiles_ref[field] = pick(choice, jnp.concatenate([old_ref[field], moved, blank], axis=0))

    row = iota((TILE, CZ), 0)
    grain = iota((TILE, CZ), 1) // TILE
    half_low = (grain - row) % 16 < 8
    row_pick = (grain - row) % 8
    lane = iota((TILE, CZ), 1)
    lane_picks = [(lane + TILE * row + 64 * half) % CZ for half in range(2)]

    def brick(index, carry):
        across, up = index // 4, index % 4
        for part in range(PARTS):
            blocks = []
            for field in range(FIELDS):
                lanes = slice(part * CZ, (part + 1) * CZ)
                first = tiles_ref[field, pl.ds(pl.multiple_of(index * 16, 16), 8), lanes]
                second = tiles_ref[field, pl.ds(pl.multiple_of(index * 16 + 8, 8), 8), lanes]
                blocks.append(grains(first, second, half_low, row_pick, lane_picks))
            for half in range(2):
                density, mom_x, mom_y, mom_z, energy = [blocks[field][half] for field in range(FIELDS)]
                inverse = 1.0 / density
                vel = [mom_x * inverse, mom_y * inverse, mom_z * inverse]
                square_sum = vel[0] * vel[0] + vel[1] * vel[1] + vel[2] * vel[2]
                pressure = (1.4 - 1.0) * (energy - 0.5 * density * square_sum)
                cell_x = across * TILE + part * 2 + half
                for field in range(FIELDS):
                    start = pl.multiple_of((field * CX + cell_x) * CY + up * TILE, TILE)
                    state_ref[pl.ds(start, TILE), :] = blocks[field][half]
                    prim_ref[pl.ds(start, TILE), :] = density if field == 0 else (
                        pressure if field == 4 else vel[field - 1]
                    )
        return carry

    lax.fori_loop(0, 8, brick, 0)
    for field in range(FIELDS):
        x_low_ref[pl.ds(field * 96, 96), :] = prim_ref[pl.ds(field * CX * CY, 96), :]
        x_high_ref[pl.ds(field * 96, 96), :] = prim_ref[pl.ds((field * CX + 13) * CY, 96), :]
        for layer in range(3):
            for block in range(2):
                start = (field * CX + block * 8) * CY
                rows = pl.ds((field * 3 + layer) * CX + block * 8, 8)
                y_low_ref[rows, :] = prim_ref[pl.ds(start + layer, 8, stride=CY), :]
                y_high_ref[rows, :] = prim_ref[pl.ds(start + CY - 3 + layer, 8, stride=CY), :]


def unpack(me, pos, old, near, half, far):
    vmem = pl.BlockSpec(memory_space=pltpu.VMEM)
    grid_rows = jax.ShapeDtypeStruct((ROWS, CZ), jnp.float32)
    x_side = jax.ShapeDtypeStruct((FIELDS * 3 * CY, CZ), jnp.float32)
    y_side = jax.ShapeDtypeStruct((FIELDS * 3 * CX, CZ), jnp.float32)
    return pl.pallas_call(
        unpack_kernel,
        out_shape=(grid_rows, grid_rows, x_side, x_side, y_side, y_side),
        in_specs=[pl.BlockSpec(memory_space=pltpu.SMEM)] + [vmem] * 5,
        out_specs=(vmem,) * 6,
        scratch_shapes=[pltpu.VMEM((FIELDS, TILES, CELLS), jnp.float32)],
        compiler_params=pltpu.CompilerParams(vmem_limit_bytes=VMEM_LIMIT),
        name="unpack",
    )(me, pos, old, near, half, far)


def median_zero(first_value, second_value):
    return jnp.maximum(
        jnp.minimum(first_value, 0.0), jnp.minimum(jnp.maximum(first_value, 0.0), second_value)
    )


def interface(prev, here, after, far):
    value = 7.0 / 12.0 * (here + after) - 1.0 / 12.0 * (prev + far)
    return jnp.minimum(jnp.maximum(value, jnp.minimum(here, after)), jnp.maximum(here, after))


def edges(centre, below, above):
    low, high = below - centre, above - centre
    return centre + median_zero(low, -2.0 * high), centre + median_zero(high, -2.0 * low)


def face_flux(left, right, normal):
    def speeds(side):
        scaled = 1.4 * side[4]
        sound = scaled * lax.rsqrt(scaled * side[0])
        return side[normal] - sound, side[normal] + sound

    left_low, left_high = speeds(left)
    right_low, right_high = speeds(right)
    slowest = jnp.minimum(jnp.minimum(left_low, right_low), 0.0)
    fastest = jnp.maximum(jnp.maximum(left_high, right_high), 0.0)
    inverse = 1.0 / (fastest - slowest)
    share_left = fastest * inverse
    share_right = -slowest * inverse
    spread = slowest * share_left
    rate_left = share_left * left[normal] - spread
    rate_right = share_right * right[normal] + spread
    mass_left, mass_right = rate_left * left[0], rate_right * right[0]
    push_left, push_right = share_left * left[4], share_right * right[4]
    flux = [mass_left + mass_right]
    for axis in range(1, 4):
        value = mass_left * left[axis] + mass_right * right[axis]
        if axis == normal:
            value = value + (push_left + push_right)
        flux.append(value)

    def carried(side, rate, mass, push):
        speed_square = side[1] * side[1] + side[2] * side[2] + side[3] * side[3]
        return 2.5 * (rate * side[4]) + 0.5 * (mass * speed_square) + push * side[normal]

    flux.append(
        carried(left, rate_left, mass_left, push_left) + carried(right, rate_right, mass_right, push_right)
    )
    return flux


def sweep(load, count, normal, emit):
    every = range(FIELDS)
    cells = {cell: load(cell) for cell in (-3, -2, -1, 0)}
    below = [interface(cells[-3][f], cells[-2][f], cells[-1][f], cells[0][f]) for f in every]
    left = flux_below = None
    for cell in range(-1, count + 1):
        cells[cell + 2] = load(cell + 2)
        above = [
            interface(cells[cell - 1][f], cells[cell][f], cells[cell + 1][f], cells[cell + 2][f]) for f in every
        ]
        pairs = [edges(cells[cell][f], below[f], above[f]) for f in every]
        if left is not None:
            flux = face_flux(left, [pair[0] for pair in pairs], normal)
            if flux_below is not None:
                emit(cell - 1, [flux[f] - flux_below[f] for f in every])
            flux_below = flux
        left = [pair[1] for pair in pairs]
        below = above


def z_kernel(state_ref, prim_ref, out_ref):
    def rolled(value, shift):
        return pltpu.roll(value, shift % CZ, 1)

    def step(cell_x, carry):
        for up in range(CY // 8):
            starts = [
                pl.multiple_of((f * CX + cell_x) * CY + up * 8, 8) for f in range(FIELDS)
            ]
            here = [prim_ref[pl.ds(start, 8), :] for start in starts]
            lows, highs = [], []
            for value in here:
                after = rolled(value, -1)
                above = interface(rolled(value, 1), value, after, rolled(after, -1))
                low, high = edges(value, rolled(above, 1), above)
                lows.append(rolled(low, -1))
                highs.append(high)
            flux = face_flux(highs, lows, 3)
            for f in range(FIELDS):
                change = flux[f] - rolled(flux[f], 1)
                out_ref[pl.ds(starts[f], 8), :] = state_ref[pl.ds(starts[f], 8), :] - 0.1 * change
        return carry

    lax.fori_loop(0, CX, step, 0)


def y_kernel(before_ref, prim_ref, low_ref, high_ref, out_ref):
    def step(block, carry):
        def load(cell):
            if cell < 0 or cell >= CY:
                ref, layer = (low_ref, cell + 3) if cell < 0 else (high_ref, cell - CY)
                return [
                    ref[pl.ds(pl.multiple_of((f * 3 + layer) * CX + block * 8, 8), 8), :] for f in range(FIELDS)
                ]
            return [prim_ref[pl.ds((f * CX + block * 8) * CY + cell, 8, stride=CY), :] for f in range(FIELDS)]

        def emit(cell, change):
            for f in range(FIELDS):
                rows = pl.ds((f * CX + block * 8) * CY + cell, 8, stride=CY)
                out_ref[rows, :] = before_ref[rows, :] - 0.1 * change[f]

        sweep(load, CY, 2, emit)
        return carry

    lax.fori_loop(0, CX // 8, step, 0)


def x_kernel(before_ref, prim_ref, low_ref, high_ref, out_ref):
    def step(block, carry):
        def load(cell):
            if cell < 0 or cell >= CX:
                ref, layer = (low_ref, cell + 3) if cell < 0 else (high_ref, cell - CX)
                return [
                    ref[pl.ds(pl.multiple_of((f * 3 + layer) * CY + block * 8, 8), 8), :] for f in range(FIELDS)
                ]
            return [
                prim_ref[pl.ds(pl.multiple_of((f * CX + cell) * CY + block * 8, 8), 8), :] for f in range(FIELDS)
            ]

        def emit(cell, change):
            for f in range(FIELDS):
                rows = pl.ds(pl.multiple_of((f * CX + cell) * CY + block * 8, 8), 8)
                out_ref[rows, :] = before_ref[rows, :] - 0.1 * change[f]

        sweep(load, CX, 1, emit)
        return carry

    lax.fori_loop(0, CY // 8, step, 0)


def stage(kernel, name, *operands):
    vmem = pl.BlockSpec(memory_space=pltpu.VMEM)
    return pl.pallas_call(
        kernel,
        out_shape=jax.ShapeDtypeStruct((ROWS, CZ), jnp.float32),
        in_specs=[vmem] * len(operands),
        out_specs=vmem,
        compiler_params=pltpu.CompilerParams(vmem_limit_bytes=VMEM_LIMIT),
        cost_estimate=pl.CostEstimate(flops=20_000_000, bytes_accessed=4_000_000, transcendentals=200_000),
        name=name,
    )(*operands)


def shifted(value, axes, count, target):
    pairs = [(i, target(i)) for i in range(count)]
    return lax.ppermute(value, axes, [pair for pair in pairs if 0 <= pair[1] < count])


def next_node(device):
    node, dev = device // 8, device % 8
    return (node + (1 if dev >= 4 else -1)) * 8 + dev


def body(old_state, old_tile_pos):
    dev = lax.axis_index("dev")
    me = (lax.axis_index("node") * 8 + dev).astype(jnp.int32).reshape(1)
    pos = old_tile_pos.reshape(1, TILES)
    old = old_state.transpose(1, 0, 2)
    near, half, far, relay = pack(me, pos, old)
    relay = shifted(relay, AXES, 128, next_node)
    half = shifted(half, AXES, 128, lambda device: device ^ 4)
    far = shifted(far, AXES, 128, lambda device: device ^ 64)
    blank = jnp.zeros_like(relay)
    near = near + jnp.concatenate([jnp.where(dev >= 4, relay, blank), jnp.where(dev < 4, relay, blank)], axis=0)
    near = lax.all_to_all(near, "dev", split_axis=0, concat_axis=0, tiled=True)
    state, prim, x_low, x_high, y_low, y_high = unpack(me, pos, old, near, half, far)
    y_before = shifted(y_high, "dev", 8, lambda i: (i + 1) % 8)
    y_after = shifted(y_low, "dev", 8, lambda i: (i - 1) % 8)
    x_before = shifted(x_high, "node", 16, lambda i: (i + 1) % 16)
    x_after = shifted(x_low, "node", 16, lambda i: (i - 1) % 16)
    result = stage(z_kernel, "flux_third", state, prim)
    result = stage(y_kernel, "flux_second", result, prim, y_before, y_after)
    result = stage(x_kernel, "flux_first", result, prim, x_before, x_after)
    return result.reshape(FIELDS, CX, CY, CZ)


def solution(mesh):
    in_specs = (P(AXES, None, None), P(AXES))
    out_specs = P(None, "node", "dev", None)
    return jax.shard_map(body, mesh=mesh, in_specs=in_specs, out_specs=out_specs, check_vma=False)
```

```python
import jax
import jax.numpy as jnp
from jax import lax
from jax.experimental import pallas as pl
from jax.experimental.pallas import tpu as pltpu
from jax.sharding import PartitionSpec as P

CX = 16
CY = 32
CZ = 128
FIELDS = 5
TILE = 8
MOVE = 8
TILES = 128
CELLS = 512
PARTS = CELLS // CZ
PLANES = FIELDS * PARTS + 1
ROWS = FIELDS * CX * CY
VMEM_LIMIT = 48 * 1024 * 1024

EARLY_FAR = 3 * MOVE
EARLY_RELAY = 4 * MOVE
EARLY_ROWS = 8 * MOVE
LATE_ROWS = 4 * MOVE
ARRIVED = 9 * MOVE

AXES = ("node", "dev")


def iota(shape, dim):
    return lax.broadcasted_iota(jnp.int32, shape, dim)


def split3(value):
    high = value.astype(jnp.bfloat16)
    rest = value - high.astype(jnp.float32)
    mid = rest.astype(jnp.bfloat16)
    low = (rest - mid.astype(jnp.float32)).astype(jnp.bfloat16)
    return high, mid, low


def pick(choice, values):
    total = None
    for part in reversed(split3(values)):
        term = jnp.dot(choice, part, preferred_element_type=jnp.float32)
        total = term if total is None else total + term
    return total


def place():
    return lax.axis_index("node"), lax.axis_index("dev")


def targets(pos):
    square = (TILES, TILES)
    by_lane = jnp.broadcast_to(pos // TILES, square)
    by_row = by_lane.T
    earlier = (by_lane == by_row) & (iota(square, 0) < iota(square, 1))
    rank = jnp.sum(earlier.astype(jnp.int32), axis=0, keepdims=True)
    return pos // TILES, pos % TILES, rank


def packed(target, local, rows, old_ref, put):
    shape = (rows, TILES)
    chosen = iota(shape, 0) == jnp.broadcast_to(target, shape)
    code = jnp.sum(
        jnp.where(chosen, jnp.broadcast_to(local + 1, shape), 0).astype(jnp.float32), axis=1, keepdims=True
    )
    put(PLANES - 1, jnp.broadcast_to(code, shape))
    choice = chosen.astype(jnp.float32).astype(jnp.bfloat16)
    for field in range(FIELDS):
        values = pick(choice, old_ref[field])
        for part in range(PARTS):
            put(field * PARTS + part, values[:, part * CZ : (part + 1) * CZ])


def pack_early_kernel(pos_ref, old_ref, one_ref, two_ref, three_ref, far_ref, relay_ref):
    node, dev = place()
    owner, local, rank = targets(pos_ref[...])
    mask = (owner % 8) ^ dev
    inside = jnp.where((mask >= 1) & (mask < 4), (mask - 1) * MOVE + rank, -1)
    outside = jnp.where(owner // 8 == node ^ 8, EARLY_FAR, EARLY_RELAY + (mask - 4) * MOVE) + rank
    target = jnp.where(owner // 8 == node, inside, outside)

    def put(plane, value):
        for block, ref in enumerate((one_ref, two_ref, three_ref, far_ref)):
            ref[plane] = value[block * MOVE : (block + 1) * MOVE]
        for block in range(4):
            first = EARLY_RELAY + block * MOVE
            relay_ref[block, plane] = value[first : first + MOVE]

    packed(target, local, EARLY_ROWS, old_ref, put)


def pack_late_kernel(
    pos_ref, old_ref, relay_ref, one_ref, two_ref, three_ref, far_ref, four_ref, five_ref, six_ref, seven_ref
):
    node, dev = place()
    owner, local, rank = targets(pos_ref[...])
    mask = (owner % 8) ^ dev
    target = jnp.where((owner // 8 == node) & (mask >= 4), (mask - 4) * MOVE + rank, -1)

    def put(plane, value):
        four_ref[0, plane] = value[:MOVE]
        four_ref[1, plane] = relay_ref[0, plane]
        for block, ref in enumerate((five_ref, six_ref, seven_ref), 1):
            ref[plane] = value[block * MOVE : (block + 1) * MOVE] + relay_ref[block, plane]

    packed(target, local, LATE_ROWS, old_ref, put)


VMEM = pl.BlockSpec(memory_space=pltpu.VMEM)
ANYWHERE = pl.BlockSpec(memory_space=pl.ANY)
BUFFER = jax.ShapeDtypeStruct((PLANES, MOVE, CZ), jnp.float32)


def buffers(count):
    return jax.ShapeDtypeStruct((count,) + BUFFER.shape, jnp.float32)


def call(kernel, name, out_shape, in_specs, **more):
    return pl.pallas_call(
        kernel,
        out_shape=out_shape,
        in_specs=in_specs,
        out_specs=jax.tree.map(lambda _: VMEM, out_shape),
        compiler_params=pltpu.CompilerParams(vmem_limit_bytes=VMEM_LIMIT),
        name=name,
        **more,
    )


def pack_early(pos, old):
    return call(pack_early_kernel, "pack_early", (BUFFER,) * 4 + (buffers(4),), [VMEM, VMEM])(pos, old)


def pack_late(pos, old, relay, *before):
    return call(
        pack_late_kernel, "pack_late", (buffers(2),) + (BUFFER,) * 3, [VMEM] * 3 + [ANYWHERE] * 4
    )(pos, old, relay, *before)


def grains(first, second, half_low, row_pick, lane_picks):
    first = pltpu.roll(first, 0, 1, stride=TILE, stride_axis=0)
    second = pltpu.roll(second, 64, 1, stride=TILE, stride_axis=0)
    result = []
    for half in range(2):
        mixed = jnp.where(half_low, first, second) if half == 0 else jnp.where(half_low, second, first)
        mixed = jnp.take_along_axis(mixed, row_pick, axis=0)
        result.append(jnp.take_along_axis(mixed, lane_picks[half], axis=1))
    return result


def unpack_kernel(
    pos_ref, old_ref, one_ref, two_ref, three_ref, far_ref, four_ref, five_ref, six_ref, seven_ref,
    state_ref, prim_ref, x_first_ref, x_second_ref, y_first_ref, y_second_ref, tiles_ref,
):
    node, dev = place()
    pos = pos_ref[...]
    square = (TILES, TILES)
    kept = jnp.where(pos // TILES == node * 8 + dev, pos % TILES, -1)
    kept_choice = jnp.broadcast_to(kept, square) == iota(square, 0)

    def arrived(plane):
        refs = (one_ref, two_ref, three_ref, far_ref, five_ref, six_ref, seven_ref)
        return jnp.concatenate([ref[plane] for ref in refs] + [four_ref[0, plane], four_ref[1, plane]], axis=0)

    code = jnp.concatenate([arrived(PLANES - 1), jnp.zeros((TILES - ARRIVED, CZ), jnp.float32)], axis=0)
    code = code.T.astype(jnp.int32)
    new_choice = code == iota(square, 0) + 1
    choice = jnp.concatenate([kept_choice, new_choice], axis=1).astype(jnp.float32).astype(jnp.bfloat16)
    blank = jnp.zeros((TILES - ARRIVED, CELLS), jnp.float32)
    for field in range(FIELDS):
        moved = jnp.concatenate([arrived(field * PARTS + part) for part in range(PARTS)], axis=1)
        tiles_ref[field] = pick(choice, jnp.concatenate([old_ref[field], moved, blank], axis=0))

    row = iota((TILE, CZ), 0)
    grain = iota((TILE, CZ), 1) // TILE
    half_low = (grain - row) % 16 < 8
    row_pick = (grain - row) % 8
    lane = iota((TILE, CZ), 1)
    lane_picks = [(lane + TILE * row + 64 * half) % CZ for half in range(2)]

    def brick(index, carry):
        across, up = index // 4, index % 4
        for part in range(PARTS):
            blocks = []
            for field in range(FIELDS):
                lanes = slice(part * CZ, (part + 1) * CZ)
                first = tiles_ref[field, pl.ds(pl.multiple_of(index * 16, 16), 8), lanes]
                second = tiles_ref[field, pl.ds(pl.multiple_of(index * 16 + 8, 8), 8), lanes]
                blocks.append(grains(first, second, half_low, row_pick, lane_picks))
            for half in range(2):
                density, mom_x, mom_y, mom_z, energy = [blocks[field][half] for field in range(FIELDS)]
                inverse = 1.0 / density
                vel = [mom_x * inverse, mom_y * inverse, mom_z * inverse]
                square_sum = vel[0] * vel[0] + vel[1] * vel[1] + vel[2] * vel[2]
                pressure = (1.4 - 1.0) * (energy - 0.5 * density * square_sum)
                cell_x = across * TILE + part * 2 + half
                for field in range(FIELDS):
                    start = pl.multiple_of((field * CX + cell_x) * CY + up * TILE, TILE)
                    state_ref[pl.ds(start, TILE), :] = blocks[field][half]
                    prim_ref[pl.ds(start, TILE), :] = density if field == 0 else (
                        pressure if field == 4 else vel[field - 1]
                    )
        return carry

    lax.fori_loop(0, 8, brick, 0)
    x_odd, y_odd = node % 2 == 1, dev % 2 == 1
    x_last, y_last = (CX - 3) * CY, CY - 3
    for odd_x, odd_y, x_ref, y_ref in (
        (x_odd, y_odd, x_first_ref, y_first_ref),
        (~x_odd, ~y_odd, x_second_ref, y_second_ref),
    ):
        x_start = pl.multiple_of(jnp.where(odd_x, 0, x_last), TILE)
        y_start = jnp.where(odd_y, 0, y_last)
        for field in range(FIELDS):
            x_ref[pl.ds(field * 96, 96), :] = prim_ref[pl.ds(field * CX * CY + x_start, 96), :]
            for layer in range(3):
                for block in range(2):
                    start = (field * CX + block * 8) * CY + layer
                    rows = pl.ds((field * 3 + layer) * CX + block * 8, 8)
                    y_ref[rows, :] = prim_ref[pl.ds(start + y_start, 8, stride=CY), :]


def unpack(*operands):
    grid_rows = jax.ShapeDtypeStruct((ROWS, CZ), jnp.float32)
    x_side = jax.ShapeDtypeStruct((FIELDS * 3 * CY, CZ), jnp.float32)
    y_side = jax.ShapeDtypeStruct((FIELDS * 3 * CX, CZ), jnp.float32)
    return call(
        unpack_kernel,
        "unpack",
        (grid_rows, grid_rows, x_side, x_side, y_side, y_side),
        [VMEM] * len(operands),
        scratch_shapes=[pltpu.VMEM((FIELDS, TILES, CELLS), jnp.float32)],
    )(*operands)


def median_zero(first_value, second_value):
    return jnp.maximum(
        jnp.minimum(first_value, 0.0), jnp.minimum(jnp.maximum(first_value, 0.0), second_value)
    )


def interface(prev, here, after, far):
    value = 7.0 / 12.0 * (here + after) - 1.0 / 12.0 * (prev + far)
    return jnp.minimum(jnp.maximum(value, jnp.minimum(here, after)), jnp.maximum(here, after))


def edges(centre, below, above):
    low, high = below - centre, above - centre
    return centre + median_zero(low, -2.0 * high), centre + median_zero(high, -2.0 * low)


def face_flux(left, right, normal):
    def speeds(side):
        scaled = 1.4 * side[4]
        sound = scaled * lax.rsqrt(scaled * side[0])
        return side[normal] - sound, side[normal] + sound

    left_low, left_high = speeds(left)
    right_low, right_high = speeds(right)
    slowest = jnp.minimum(jnp.minimum(left_low, right_low), 0.0)
    fastest = jnp.maximum(jnp.maximum(left_high, right_high), 0.0)
    inverse = 1.0 / (fastest - slowest)
    share_left = fastest * inverse
    share_right = -slowest * inverse
    spread = slowest * share_left
    rate_left = share_left * left[normal] - spread
    rate_right = share_right * right[normal] + spread
    mass_left, mass_right = rate_left * left[0], rate_right * right[0]
    push_left, push_right = share_left * left[4], share_right * right[4]
    flux = [mass_left + mass_right]
    for axis in range(1, 4):
        value = mass_left * left[axis] + mass_right * right[axis]
        if axis == normal:
            value = value + (push_left + push_right)
        flux.append(value)

    def carried(side, rate, mass, push):
        speed_square = side[1] * side[1] + side[2] * side[2] + side[3] * side[3]
        return 2.5 * (rate * side[4]) + 0.5 * (mass * speed_square) + push * side[normal]

    flux.append(
        carried(left, rate_left, mass_left, push_left) + carried(right, rate_right, mass_right, push_right)
    )
    return flux


def sweep(load, count, normal, emit):
    every = range(FIELDS)
    cells = {cell: load(cell) for cell in (-3, -2, -1, 0)}
    below = [interface(cells[-3][f], cells[-2][f], cells[-1][f], cells[0][f]) for f in every]
    left = flux_below = None
    for cell in range(-1, count + 1):
        cells[cell + 2] = load(cell + 2)
        above = [
            interface(cells[cell - 1][f], cells[cell][f], cells[cell + 1][f], cells[cell + 2][f]) for f in every
        ]
        pairs = [edges(cells[cell][f], below[f], above[f]) for f in every]
        if left is not None:
            flux = face_flux(left, [pair[0] for pair in pairs], normal)
            if flux_below is not None:
                emit(cell - 1, [flux[f] - flux_below[f] for f in every])
            flux_below = flux
        left = [pair[1] for pair in pairs]
        below = above


def z_kernel(state_ref, prim_ref, out_ref):
    def rolled(value, shift):
        return pltpu.roll(value, shift % CZ, 1)

    def step(cell_x, carry):
        for up in range(CY // 8):
            starts = [
                pl.multiple_of((f * CX + cell_x) * CY + up * 8, 8) for f in range(FIELDS)
            ]
            here = [prim_ref[pl.ds(start, 8), :] for start in starts]
            lows, highs = [], []
            for value in here:
                after = rolled(value, -1)
                above = interface(rolled(value, 1), value, after, rolled(after, -1))
                low, high = edges(value, rolled(above, 1), above)
                lows.append(rolled(low, -1))
                highs.append(high)
            flux = face_flux(highs, lows, 3)
            for f in range(FIELDS):
                change = flux[f] - rolled(flux[f], 1)
                out_ref[pl.ds(starts[f], 8), :] = state_ref[pl.ds(starts[f], 8), :] - 0.1 * change
        return carry

    lax.fori_loop(0, CX, step, 0)


def side(first_ref, second_ref, odd, before, rows):
    first, second = first_ref[rows, :], second_ref[rows, :]
    return jnp.where(odd, first, second) if before else jnp.where(odd, second, first)


def y_kernel(before_ref, prim_ref, first_ref, second_ref, out_ref):
    odd = lax.axis_index("dev") % 2 == 1

    def step(block, carry):
        def load(cell):
            if cell < 0 or cell >= CY:
                layer = cell + 3 if cell < 0 else cell - CY
                rows = [pl.ds(pl.multiple_of((f * 3 + layer) * CX + block * 8, 8), 8) for f in range(FIELDS)]
                return [side(first_ref, second_ref, odd, cell < 0, row) for row in rows]
            return [prim_ref[pl.ds((f * CX + block * 8) * CY + cell, 8, stride=CY), :] for f in range(FIELDS)]

        def emit(cell, change):
            for f in range(FIELDS):
                rows = pl.ds((f * CX + block * 8) * CY + cell, 8, stride=CY)
                out_ref[rows, :] = before_ref[rows, :] - 0.1 * change[f]

        sweep(load, CY, 2, emit)
        return carry

    lax.fori_loop(0, CX // 8, step, 0)


def x_kernel(before_ref, prim_ref, first_ref, second_ref, out_ref):
    odd = lax.axis_index("node") % 2 == 1

    def step(block, carry):
        def load(cell):
            if cell < 0 or cell >= CX:
                layer = cell + 3 if cell < 0 else cell - CX
                rows = [pl.ds(pl.multiple_of((f * 3 + layer) * CY + block * 8, 8), 8) for f in range(FIELDS)]
                return [side(first_ref, second_ref, odd, cell < 0, row) for row in rows]
            return [
                prim_ref[pl.ds(pl.multiple_of((f * CX + cell) * CY + block * 8, 8), 8), :] for f in range(FIELDS)
            ]

        def emit(cell, change):
            for f in range(FIELDS):
                rows = pl.ds(pl.multiple_of((f * CX + cell) * CY + block * 8, 8), 8)
                out_ref[rows, :] = before_ref[rows, :] - 0.1 * change[f]

        sweep(load, CX, 1, emit)
        return carry

    lax.fori_loop(0, CY // 8, step, 0)


def stage(kernel, name, *operands):
    return call(
        kernel,
        name,
        jax.ShapeDtypeStruct((ROWS, CZ), jnp.float32),
        [VMEM] * len(operands),
        cost_estimate=pl.CostEstimate(flops=20_000_000, bytes_accessed=4_000_000, transcendentals=200_000),
    )(*operands)


def shifted(value, axes, count, target):
    pairs = [(i, target(i)) for i in range(count)]
    return lax.ppermute(value, axes, [pair for pair in pairs if 0 <= pair[1] < count])


def next_node(device):
    node, dev = device // 8, device % 8
    return (node + (1 if dev >= 4 else -1)) * 8 + dev


def masked(value, mask):
    return shifted(value, AXES, 128, lambda device: device ^ mask)


def body(old_state, old_tile_pos):
    pos = old_tile_pos.reshape(1, TILES)
    old = old_state.transpose(1, 0, 2)
    one, two, three, far, relay = pack_early(pos, old)
    relay = shifted(relay, AXES, 128, next_node)
    early = (masked(one, 1), masked(two, 2), masked(three, 3), masked(far, 64))
    late = pack_late(pos, old, relay, *early)
    late = [masked(value, 4 + index) for index, value in enumerate(late)]
    state, prim, x_first, x_second, y_first, y_second = unpack(pos, old, *early, *late)
    x_first = shifted(x_first, "node", 16, lambda i: i ^ 1)
    x_second = shifted(x_second, "node", 16, lambda i: (i + 1) % 16 if i % 2 else (i - 1) % 16)
    y_first = shifted(y_first, "dev", 8, lambda i: i ^ 1)
    y_second = shifted(y_second, "dev", 8, lambda i: (i + 1) % 8 if i % 2 else (i - 1) % 8)
    result = stage(z_kernel, "flux_third", state, prim)
    result = stage(y_kernel, "flux_second", result, prim, y_first, y_second)
    result = stage(x_kernel, "flux_first", result, prim, x_first, x_second)
    return result.reshape(FIELDS, CX, CY, CZ)


def solution(mesh):
    in_specs = (P(AXES, None, None), P(AXES))
    out_specs = P(None, "node", "dev", None)
    return jax.shard_map(body, mesh=mesh, in_specs=in_specs, out_specs=out_specs, check_vma=False)
```

```python
import jax
import jax.numpy as jnp
from jax import lax
from jax.experimental import pallas as pl
from jax.experimental.pallas import tpu as pltpu
from jax.sharding import PartitionSpec as P

CX = 16
CY = 32
CZ = 128
FIELDS = 5
TILE = 8
MOVE = 8
TILES = 128
CELLS = 512
PARTS = CELLS // CZ
PLANES = FIELDS * PARTS + 1
ROWS = FIELDS * CX * CY
VMEM_LIMIT = 48 * 1024 * 1024

EARLY_RELAY = 4 * MOVE
EARLY_ROWS = 6 * MOVE
LATE_ROWS = 4 * MOVE
ARRIVED = 9 * MOVE

AXES = ("node", "dev")


def iota(shape, dim):
    return lax.broadcasted_iota(jnp.int32, shape, dim)


def split3(value):
    high = value.astype(jnp.bfloat16)
    rest = value - high.astype(jnp.float32)
    mid = rest.astype(jnp.bfloat16)
    low = (rest - mid.astype(jnp.float32)).astype(jnp.bfloat16)
    return high, mid, low


def pick(choice, values):
    total = None
    for part in reversed(split3(values)):
        term = jnp.dot(choice, part, preferred_element_type=jnp.float32)
        total = term if total is None else total + term
    return total


def place():
    return lax.axis_index("node"), lax.axis_index("dev")


def targets(pos):
    square = (TILES, TILES)
    by_lane = jnp.broadcast_to(pos // TILES, square)
    by_row = by_lane.T
    earlier = (by_lane == by_row) & (iota(square, 0) < iota(square, 1))
    rank = jnp.sum(earlier.astype(jnp.int32), axis=0, keepdims=True)
    return pos // TILES, pos % TILES, rank


def packed(target, local, rows, old_ref, put, ready=None):
    shape = (rows, TILES)
    chosen = iota(shape, 0) == jnp.broadcast_to(target, shape)
    code = jnp.sum(
        jnp.where(chosen, jnp.broadcast_to(local + 1, shape), 0).astype(jnp.float32), axis=1, keepdims=True
    )
    put(PLANES - 1, jnp.broadcast_to(code, shape))
    choice = chosen.astype(jnp.float32).astype(jnp.bfloat16)
    if ready is not None:
        ready()
    for field in range(FIELDS):
        values = pick(choice, old_ref[field])
        for part in range(PARTS):
            put(field * PARTS + part, values[:, part * CZ : (part + 1) * CZ])


def pack_early_kernel(
    pos_hbm, old_hbm, two_ref, three_ref, six_ref, seven_ref, relay_ref, pos_ref, old_ref, sems
):
    node, dev = place()
    pos_copy = pltpu.make_async_copy(pos_hbm, pos_ref, sems.at[0])
    old_copy = pltpu.make_async_copy(old_hbm, old_ref, sems.at[1])
    pos_copy.start()
    old_copy.start()
    pos_copy.wait()
    owner, local, rank = targets(pos_ref[...])
    mask = (owner % 8) ^ dev
    outer, low = mask >= 4, mask % 4
    here = owner // 8 == node
    by_mask = (mask // 4 * 2 + mask % 2) * MOVE + rank
    relayed = EARLY_RELAY + mask % 2 * MOVE + rank
    target = jnp.where(low >= 2, by_mask, jnp.where(outer & ~here, relayed, -1))
    target = jnp.where(owner // 8 == node ^ 8, -1, target)

    def put(plane, value):
        for block, ref in enumerate((two_ref, three_ref, six_ref, seven_ref)):
            ref[plane] = value[block * MOVE : (block + 1) * MOVE]
        for block in range(2):
            first = EARLY_RELAY + block * MOVE
            relay_ref[block, plane] = value[first : first + MOVE]

    packed(target, local, EARLY_ROWS, old_ref, put, old_copy.wait)


def pack_late_kernel(
    pos_ref, old_ref, relay_ref, six_ref, seven_ref, one_ref, four_ref, five_ref, far_ref, on_ref
):
    node, dev = place()
    owner, local, rank = targets(pos_ref[...])
    mask = (owner % 8) ^ dev
    inside = jnp.where((mask == 1) | (mask == 4) | (mask == 5), (mask // 4 + mask % 2) * MOVE, -TILES)
    inside = jnp.where(mask == 1, 0, inside)
    target = jnp.where(owner // 8 == node, inside, jnp.where(owner // 8 == node ^ 8, 3 * MOVE, -TILES)) + rank

    def put(plane, value):
        one_ref[plane] = value[:MOVE]
        four_ref[0, plane] = value[MOVE : 2 * MOVE]
        four_ref[1, plane] = relay_ref[0, plane]
        five_ref[plane] = value[2 * MOVE : 3 * MOVE] + relay_ref[1, plane]
        far_ref[plane] = value[3 * MOVE :]
        on_ref[0, plane] = six_ref[plane]
        on_ref[1, plane] = seven_ref[plane]

    packed(target, local, LATE_ROWS, old_ref, put)


VMEM = pl.BlockSpec(memory_space=pltpu.VMEM)
ANYWHERE = pl.BlockSpec(memory_space=pl.ANY)
HBM = pl.BlockSpec(memory_space=pltpu.HBM)
BUFFER = jax.ShapeDtypeStruct((PLANES, MOVE, CZ), jnp.float32)


def buffers(count):
    return jax.ShapeDtypeStruct((count,) + BUFFER.shape, jnp.float32)


def call(kernel, name, out_shape, in_specs, **more):
    return pl.pallas_call(
        kernel,
        out_shape=out_shape,
        in_specs=in_specs,
        out_specs=jax.tree.map(lambda _: VMEM, out_shape),
        compiler_params=pltpu.CompilerParams(vmem_limit_bytes=VMEM_LIMIT),
        name=name,
        **more,
    )


def pack_early(pos, old):
    return call(
        pack_early_kernel,
        "pack_early",
        (BUFFER,) * 4 + (buffers(2),),
        [HBM, HBM],
        scratch_shapes=[
            pltpu.VMEM(pos.shape, jnp.int32),
            pltpu.VMEM(old.shape, jnp.float32),
            pltpu.SemaphoreType.DMA((2,)),
        ],
    )(pos, old)


def pack_late(pos, old, relay, six, seven, *before):
    return call(
        pack_late_kernel,
        "pack_late",
        (BUFFER, buffers(2), BUFFER, BUFFER, buffers(2)),
        [VMEM] * 5 + [ANYWHERE] * len(before),
    )(pos, old, relay, six, seven, *before)


def grains(first, second, half_low, row_pick, lane_picks):
    first = pltpu.roll(first, 0, 1, stride=TILE, stride_axis=0)
    second = pltpu.roll(second, 64, 1, stride=TILE, stride_axis=0)
    result = []
    for half in range(2):
        mixed = jnp.where(half_low, first, second) if half == 0 else jnp.where(half_low, second, first)
        mixed = jnp.take_along_axis(mixed, row_pick, axis=0)
        result.append(jnp.take_along_axis(mixed, lane_picks[half], axis=1))
    return result


def unpack_kernel(
    pos_ref, old_ref, one_ref, two_ref, three_ref, four_ref, five_ref, six_ref, seven_ref, far_ref, on_ref,
    state_ref, prim_ref, x_first_ref, x_second_ref, y_first_ref, y_second_ref, tiles_ref,
):
    node, dev = place()
    pos = pos_ref[...]
    square = (TILES, TILES)
    kept = jnp.where(pos // TILES == node * 8 + dev, pos % TILES, -1)
    kept_choice = jnp.broadcast_to(kept, square) == iota(square, 0)
    middle = (dev >= 2) & (dev < 6)

    def arrived(plane):
        blocks = [ref[plane] for ref in (one_ref, two_ref, three_ref, five_ref, far_ref)]
        blocks += [four_ref[0, plane], four_ref[1, plane]]
        blocks.append(jnp.where(middle, six_ref[plane], on_ref[0, plane]))
        blocks.append(jnp.where(middle, seven_ref[plane], on_ref[1, plane]))
        return jnp.concatenate(blocks, axis=0)

    code = jnp.concatenate([arrived(PLANES - 1), jnp.zeros((TILES - ARRIVED, CZ), jnp.float32)], axis=0)
    code = code.T.astype(jnp.int32)
    new_choice = code == iota(square, 0) + 1
    choice = jnp.concatenate([kept_choice, new_choice], axis=1).astype(jnp.float32).astype(jnp.bfloat16)
    blank = jnp.zeros((TILES - ARRIVED, CELLS), jnp.float32)
    for field in range(FIELDS):
        moved = jnp.concatenate([arrived(field * PARTS + part) for part in range(PARTS)], axis=1)
        tiles_ref[field] = pick(choice, jnp.concatenate([old_ref[field], moved, blank], axis=0))

    row = iota((TILE, CZ), 0)
    grain = iota((TILE, CZ), 1) // TILE
    half_low = (grain - row) % 16 < 8
    row_pick = (grain - row) % 8
    lane = iota((TILE, CZ), 1)
    lane_picks = [(lane + TILE * row + 64 * half) % CZ for half in range(2)]

    def brick(index, carry):
        across, up = index // 4, index % 4
        for part in range(PARTS):
            blocks = []
            for field in range(FIELDS):
                lanes = slice(part * CZ, (part + 1) * CZ)
                first = tiles_ref[field, pl.ds(pl.multiple_of(index * 16, 16), 8), lanes]
                second = tiles_ref[field, pl.ds(pl.multiple_of(index * 16 + 8, 8), 8), lanes]
                blocks.append(grains(first, second, half_low, row_pick, lane_picks))
            for half in range(2):
                density, mom_x, mom_y, mom_z, energy = [blocks[field][half] for field in range(FIELDS)]
                inverse = 1.0 / density
                vel = [mom_x * inverse, mom_y * inverse, mom_z * inverse]
                square_sum = vel[0] * vel[0] + vel[1] * vel[1] + vel[2] * vel[2]
                pressure = (1.4 - 1.0) * (energy - 0.5 * density * square_sum)
                cell_x = across * TILE + part * 2 + half
                for field in range(FIELDS):
                    start = pl.multiple_of((field * CX + cell_x) * CY + up * TILE, TILE)
                    state_ref[pl.ds(start, TILE), :] = blocks[field][half]
                    prim_ref[pl.ds(start, TILE), :] = density if field == 0 else (
                        pressure if field == 4 else vel[field - 1]
                    )
        return carry

    lax.fori_loop(0, 8, brick, 0)
    x_odd, y_odd = node % 2 == 1, dev % 2 == 1
    x_last, y_last = (CX - 3) * CY, CY - 3
    for odd_x, odd_y, x_ref, y_ref in (
        (x_odd, y_odd, x_first_ref, y_first_ref),
        (~x_odd, ~y_odd, x_second_ref, y_second_ref),
    ):
        x_start = pl.multiple_of(jnp.where(odd_x, 0, x_last), TILE)
        y_start = jnp.where(odd_y, 0, y_last)
        for field in range(FIELDS):
            x_ref[pl.ds(field * 96, 96), :] = prim_ref[pl.ds(field * CX * CY + x_start, 96), :]
            for layer in range(3):
                for block in range(2):
                    start = (field * CX + block * 8) * CY + layer
                    rows = pl.ds((field * 3 + layer) * CX + block * 8, 8)
                    y_ref[rows, :] = prim_ref[pl.ds(start + y_start, 8, stride=CY), :]


def unpack(*operands):
    grid_rows = jax.ShapeDtypeStruct((ROWS, CZ), jnp.float32)
    x_side = jax.ShapeDtypeStruct((FIELDS * 3 * CY, CZ), jnp.float32)
    y_side = jax.ShapeDtypeStruct((FIELDS * 3 * CX, CZ), jnp.float32)
    return call(
        unpack_kernel,
        "unpack",
        (grid_rows, grid_rows, x_side, x_side, y_side, y_side),
        [VMEM] * len(operands),
        scratch_shapes=[pltpu.VMEM((FIELDS, TILES, CELLS), jnp.float32)],
    )(*operands)


def median_zero(first_value, second_value):
    return jnp.maximum(
        jnp.minimum(first_value, 0.0), jnp.minimum(jnp.maximum(first_value, 0.0), second_value)
    )


def interface(prev, here, after, far):
    value = 7.0 / 12.0 * (here + after) - 1.0 / 12.0 * (prev + far)
    return jnp.minimum(jnp.maximum(value, jnp.minimum(here, after)), jnp.maximum(here, after))


def edges(centre, below, above):
    low, high = below - centre, above - centre
    return centre + median_zero(low, -2.0 * high), centre + median_zero(high, -2.0 * low)


def face_flux(left, right, normal):
    def speeds(side):
        scaled = 1.4 * side[4]
        sound = scaled * lax.rsqrt(scaled * side[0])
        return side[normal] - sound, side[normal] + sound

    left_low, left_high = speeds(left)
    right_low, right_high = speeds(right)
    slowest = jnp.minimum(jnp.minimum(left_low, right_low), 0.0)
    fastest = jnp.maximum(jnp.maximum(left_high, right_high), 0.0)
    inverse = 1.0 / (fastest - slowest)
    share_left = fastest * inverse
    share_right = -slowest * inverse
    spread = slowest * share_left
    rate_left = share_left * left[normal] - spread
    rate_right = share_right * right[normal] + spread
    mass_left, mass_right = rate_left * left[0], rate_right * right[0]
    push_left, push_right = share_left * left[4], share_right * right[4]
    flux = [mass_left + mass_right]
    for axis in range(1, 4):
        value = mass_left * left[axis] + mass_right * right[axis]
        if axis == normal:
            value = value + (push_left + push_right)
        flux.append(value)

    def carried(side, rate, mass, push):
        speed_square = side[1] * side[1] + side[2] * side[2] + side[3] * side[3]
        return 2.5 * (rate * side[4]) + 0.5 * (mass * speed_square) + push * side[normal]

    flux.append(
        carried(left, rate_left, mass_left, push_left) + carried(right, rate_right, mass_right, push_right)
    )
    return flux


def sweep(load, count, normal, emit):
    every = range(FIELDS)
    cells = {cell: load(cell) for cell in (-3, -2, -1, 0)}
    below = [interface(cells[-3][f], cells[-2][f], cells[-1][f], cells[0][f]) for f in every]
    left = flux_below = None
    for cell in range(-1, count + 1):
        cells[cell + 2] = load(cell + 2)
        above = [
            interface(cells[cell - 1][f], cells[cell][f], cells[cell + 1][f], cells[cell + 2][f]) for f in every
        ]
        pairs = [edges(cells[cell][f], below[f], above[f]) for f in every]
        if left is not None:
            flux = face_flux(left, [pair[0] for pair in pairs], normal)
            if flux_below is not None:
                emit(cell - 1, [flux[f] - flux_below[f] for f in every])
            flux_below = flux
        left = [pair[1] for pair in pairs]
        below = above


def z_kernel(state_ref, prim_ref, out_ref):
    def rolled(value, shift):
        return pltpu.roll(value, shift % CZ, 1)

    def step(cell_x, carry):
        for up in range(CY // 8):
            starts = [
                pl.multiple_of((f * CX + cell_x) * CY + up * 8, 8) for f in range(FIELDS)
            ]
            here = [prim_ref[pl.ds(start, 8), :] for start in starts]
            lows, highs = [], []
            for value in here:
                after = rolled(value, -1)
                above = interface(rolled(value, 1), value, after, rolled(after, -1))
                low, high = edges(value, rolled(above, 1), above)
                lows.append(rolled(low, -1))
                highs.append(high)
            flux = face_flux(highs, lows, 3)
            for f in range(FIELDS):
                change = flux[f] - rolled(flux[f], 1)
                out_ref[pl.ds(starts[f], 8), :] = state_ref[pl.ds(starts[f], 8), :] - 0.1 * change
        return carry

    lax.fori_loop(0, CX, step, 0, unroll=2)


def side(first_ref, second_ref, odd, before, rows):
    first, second = first_ref[rows, :], second_ref[rows, :]
    return jnp.where(odd, first, second) if before else jnp.where(odd, second, first)


def y_kernel(before_ref, prim_ref, first_ref, second_ref, out_ref):
    odd = lax.axis_index("dev") % 2 == 1

    def step(block, carry):
        def load(cell):
            if cell < 0 or cell >= CY:
                layer = cell + 3 if cell < 0 else cell - CY
                rows = [pl.ds(pl.multiple_of((f * 3 + layer) * CX + block * 8, 8), 8) for f in range(FIELDS)]
                return [side(first_ref, second_ref, odd, cell < 0, row) for row in rows]
            return [prim_ref[pl.ds((f * CX + block * 8) * CY + cell, 8, stride=CY), :] for f in range(FIELDS)]

        def emit(cell, change):
            for f in range(FIELDS):
                rows = pl.ds((f * CX + block * 8) * CY + cell, 8, stride=CY)
                out_ref[rows, :] = before_ref[rows, :] - 0.1 * change[f]

        sweep(load, CY, 2, emit)
        return carry

    lax.fori_loop(0, CX // 8, step, 0)


def x_kernel(before_ref, prim_ref, first_ref, second_ref, out_ref):
    odd = lax.axis_index("node") % 2 == 1

    def step(block, carry):
        def load(cell):
            if cell < 0 or cell >= CX:
                layer = cell + 3 if cell < 0 else cell - CX
                rows = [pl.ds(pl.multiple_of((f * 3 + layer) * CY + block * 8, 8), 8) for f in range(FIELDS)]
                return [side(first_ref, second_ref, odd, cell < 0, row) for row in rows]
            return [
                prim_ref[pl.ds(pl.multiple_of((f * CX + cell) * CY + block * 8, 8), 8), :] for f in range(FIELDS)
            ]

        def emit(cell, change):
            for f in range(FIELDS):
                rows = pl.ds(pl.multiple_of((f * CX + cell) * CY + block * 8, 8), 8)
                out_ref[rows, :] = before_ref[rows, :] - 0.1 * change[f]

        sweep(load, CX, 1, emit)
        return carry

    lax.fori_loop(0, CY // 8, step, 0)


def stage(kernel, name, *operands):
    return call(
        kernel,
        name,
        jax.ShapeDtypeStruct((ROWS, CZ), jnp.float32),
        [VMEM] * len(operands),
        cost_estimate=pl.CostEstimate(flops=20_000_000, bytes_accessed=4_000_000, transcendentals=200_000),
    )(*operands)


def shifted(value, axes, count, target):
    pairs = [(i, target(i)) for i in range(count)]
    return lax.ppermute(value, axes, [pair for pair in pairs if 0 <= pair[1] < count])


def next_node(device):
    node, dev = device // 8, device % 8
    return (node + (1 if dev >= 4 else -1)) * 8 + dev


def onward_node(device):
    node, dev = device // 8, device % 8
    return -1 if 2 <= dev < 6 else (node + (1 if dev < 2 else -1)) * 8 + dev


def masked(value, mask):
    return shifted(value, AXES, 128, lambda device: device ^ mask)


def body(old_state, old_tile_pos):
    pos = old_tile_pos.reshape(1, TILES)
    old = old_state.transpose(1, 0, 2)
    two, three, six, seven, relay = pack_early(pos, old)
    relay = shifted(relay, AXES, 128, next_node)
    six, seven, two, three = masked(six, 6), masked(seven, 7), masked(two, 2), masked(three, 3)
    one, four, five, far, onward = pack_late(pos, old, relay, six, seven)
    onward = shifted(onward, AXES, 128, onward_node)
    four, five, one, far = masked(four, 4), masked(five, 5), masked(one, 1), masked(far, 64)
    state, prim, x_first, x_second, y_first, y_second = unpack(
        pos, old, one, two, three, four, five, six, seven, far, onward
    )
    x_first = shifted(x_first, "node", 16, lambda i: i ^ 1)
    x_second = shifted(x_second, "node", 16, lambda i: (i + 1) % 16 if i % 2 else (i - 1) % 16)
    y_first = shifted(y_first, "dev", 8, lambda i: i ^ 1)
    y_second = shifted(y_second, "dev", 8, lambda i: (i + 1) % 8 if i % 2 else (i - 1) % 8)
    result = stage(z_kernel, "flux_third", state, prim)
    result = stage(y_kernel, "flux_second", result, prim, y_first, y_second)
    result = stage(x_kernel, "flux_first", result, prim, x_first, x_second)
    return result.reshape(FIELDS, CX, CY, CZ)


def solution(mesh):
    in_specs = (P(AXES, None, None), P(AXES))
    out_specs = P(None, "node", "dev", None)
    return jax.shard_map(body, mesh=mesh, in_specs=in_specs, out_specs=out_specs, check_vma=False)
```

```python
import jax
import jax.numpy as jnp
from jax import lax
from jax.experimental import pallas as pl
from jax.experimental.pallas import tpu as pltpu
from jax.sharding import PartitionSpec as P

CX = 16
CY = 32
CZ = 128
FIELDS = 5
TILE = 8
MOVE = 8
TILES = 128
CELLS = 512
PARTS = CELLS // CZ
PLANES = FIELDS * PARTS + 1
ROWS = FIELDS * CX * CY
VMEM_LIMIT = 48 * 1024 * 1024

EARLY_RELAY = 4 * MOVE
EARLY_ROWS = 6 * MOVE
LATE_ROWS = 4 * MOVE
ARRIVED = 9 * MOVE

AXES = ("node", "dev")


def iota(shape, dim):
    return lax.broadcasted_iota(jnp.int32, shape, dim)


def split3(value):
    high = value.astype(jnp.bfloat16)
    rest = value - high.astype(jnp.float32)
    mid = rest.astype(jnp.bfloat16)
    low = (rest - mid.astype(jnp.float32)).astype(jnp.bfloat16)
    return high, mid, low


def pick(choice, values):
    total = None
    for part in reversed(split3(values)):
        term = jnp.dot(choice, part, preferred_element_type=jnp.float32)
        total = term if total is None else total + term
    return total


def place():
    return lax.axis_index("node"), lax.axis_index("dev")


def targets(pos):
    square = (TILES, TILES)
    by_lane = jnp.broadcast_to(pos // TILES, square)
    by_row = by_lane.T
    earlier = (by_lane == by_row) & (iota(square, 0) < iota(square, 1))
    rank = jnp.sum(earlier.astype(jnp.int32), axis=0, keepdims=True)
    return pos // TILES, pos % TILES, rank


def packed(target, local, rows, old_ref, put):
    shape = (rows, TILES)
    chosen = iota(shape, 0) == jnp.broadcast_to(target, shape)
    code = jnp.sum(
        jnp.where(chosen, jnp.broadcast_to(local + 1, shape), 0).astype(jnp.float32), axis=1, keepdims=True
    )
    put(PLANES - 1, jnp.broadcast_to(code, shape))
    choice = chosen.astype(jnp.float32).astype(jnp.bfloat16)
    for field in range(FIELDS):
        values = pick(choice, old_ref[field])
        for part in range(PARTS):
            put(field * PARTS + part, values[:, part * CZ : (part + 1) * CZ])


def pack_early_kernel(pos_ref, old_ref, two_ref, three_ref, six_ref, seven_ref, relay_ref):
    node, dev = place()
    owner, local, rank = targets(pos_ref[...])
    mask = (owner % 8) ^ dev
    outer, low = mask >= 4, mask % 4
    here = owner // 8 == node
    by_mask = (mask // 4 * 2 + mask % 2) * MOVE + rank
    relayed = EARLY_RELAY + mask % 2 * MOVE + rank
    target = jnp.where(low >= 2, by_mask, jnp.where(outer & ~here, relayed, -1))
    target = jnp.where(owner // 8 == node ^ 8, -1, target)

    def put(plane, value):
        for block, ref in enumerate((two_ref, three_ref, six_ref, seven_ref)):
            ref[plane] = value[block * MOVE : (block + 1) * MOVE]
        for block in range(2):
            first = EARLY_RELAY + block * MOVE
            relay_ref[block, plane] = value[first : first + MOVE]

    packed(target, local, EARLY_ROWS, old_ref, put)


def pack_late_kernel(
    pos_ref, old_ref, relay_ref, six_ref, seven_ref, one_ref, four_ref, five_ref, far_ref, on_ref
):
    node, dev = place()
    owner, local, rank = targets(pos_ref[...])
    mask = (owner % 8) ^ dev
    inside = jnp.where((mask == 1) | (mask == 4) | (mask == 5), (mask // 4 + mask % 2) * MOVE, -TILES)
    inside = jnp.where(mask == 1, 0, inside)
    target = jnp.where(owner // 8 == node, inside, jnp.where(owner // 8 == node ^ 8, 3 * MOVE, -TILES)) + rank

    def put(plane, value):
        one_ref[plane] = value[:MOVE]
        four_ref[0, plane] = value[MOVE : 2 * MOVE]
        four_ref[1, plane] = relay_ref[0, plane]
        five_ref[plane] = value[2 * MOVE : 3 * MOVE] + relay_ref[1, plane]
        far_ref[plane] = value[3 * MOVE :]
        on_ref[0, plane] = six_ref[plane]
        on_ref[1, plane] = seven_ref[plane]

    packed(target, local, LATE_ROWS, old_ref, put)


VMEM = pl.BlockSpec(memory_space=pltpu.VMEM)
BUFFER = jax.ShapeDtypeStruct((PLANES, MOVE, CZ), jnp.float32)


def buffers(count):
    return jax.ShapeDtypeStruct((count,) + BUFFER.shape, jnp.float32)


def call(kernel, name, out_shape, in_specs, **more):
    return pl.pallas_call(
        kernel,
        out_shape=out_shape,
        in_specs=in_specs,
        out_specs=jax.tree.map(lambda _: VMEM, out_shape),
        compiler_params=pltpu.CompilerParams(vmem_limit_bytes=VMEM_LIMIT),
        name=name,
        **more,
    )


def pack_early(pos, old):
    return call(pack_early_kernel, "pack_early", (BUFFER,) * 4 + (buffers(2),), [VMEM, VMEM])(pos, old)


def pack_late(pos, old, relay, six, seven):
    return call(
        pack_late_kernel, "pack_late", (BUFFER, buffers(2), BUFFER, BUFFER, buffers(2)), [VMEM] * 5
    )(pos, old, relay, six, seven)


def grains(first, second, half_low, row_pick, lane_picks):
    first = pltpu.roll(first, 0, 1, stride=TILE, stride_axis=0)
    second = pltpu.roll(second, 64, 1, stride=TILE, stride_axis=0)
    result = []
    for half in range(2):
        mixed = jnp.where(half_low, first, second) if half == 0 else jnp.where(half_low, second, first)
        mixed = jnp.take_along_axis(mixed, row_pick, axis=0)
        result.append(jnp.take_along_axis(mixed, lane_picks[half], axis=1))
    return result


def unpack_kernel(
    pos_ref, old_ref, one_ref, two_ref, three_ref, four_ref, five_ref, far_ref, on_ref,
    state_ref, prim_ref, x_first_ref, x_second_ref, y_first_ref, y_second_ref, tiles_ref,
):
    node, dev = place()
    pos = pos_ref[...]
    square = (TILES, TILES)
    kept = jnp.where(pos // TILES == node * 8 + dev, pos % TILES, -1)
    kept_choice = jnp.broadcast_to(kept, square) == iota(square, 0)

    def arrived(plane):
        blocks = [ref[plane] for ref in (one_ref, two_ref, three_ref, five_ref, far_ref)]
        blocks += [four_ref[0, plane], four_ref[1, plane]]
        blocks += [on_ref[0, plane], on_ref[1, plane]]
        return jnp.concatenate(blocks, axis=0)

    code = jnp.concatenate([arrived(PLANES - 1), jnp.zeros((TILES - ARRIVED, CZ), jnp.float32)], axis=0)
    code = code.T.astype(jnp.int32)
    new_choice = code == iota(square, 0) + 1
    choice = jnp.concatenate([kept_choice, new_choice], axis=1).astype(jnp.float32).astype(jnp.bfloat16)
    blank = jnp.zeros((TILES - ARRIVED, CELLS), jnp.float32)
    for field in range(FIELDS):
        moved = jnp.concatenate([arrived(field * PARTS + part) for part in range(PARTS)], axis=1)
        tiles_ref[field] = pick(choice, jnp.concatenate([old_ref[field], moved, blank], axis=0))

    row = iota((TILE, CZ), 0)
    grain = iota((TILE, CZ), 1) // TILE
    half_low = (grain - row) % 16 < 8
    row_pick = (grain - row) % 8
    lane = iota((TILE, CZ), 1)
    lane_picks = [(lane + TILE * row + 64 * half) % CZ for half in range(2)]

    def brick(index, carry):
        across, up = index // 4, index % 4
        for part in range(PARTS):
            blocks = []
            for field in range(FIELDS):
                lanes = slice(part * CZ, (part + 1) * CZ)
                first = tiles_ref[field, pl.ds(pl.multiple_of(index * 16, 16), 8), lanes]
                second = tiles_ref[field, pl.ds(pl.multiple_of(index * 16 + 8, 8), 8), lanes]
                blocks.append(grains(first, second, half_low, row_pick, lane_picks))
            for half in range(2):
                density, mom_x, mom_y, mom_z, energy = [blocks[field][half] for field in range(FIELDS)]
                inverse = 1.0 / density
                vel = [mom_x * inverse, mom_y * inverse, mom_z * inverse]
                square_sum = vel[0] * vel[0] + vel[1] * vel[1] + vel[2] * vel[2]
                pressure = (1.4 - 1.0) * (energy - 0.5 * density * square_sum)
                cell_x = across * TILE + part * 2 + half
                for field in range(FIELDS):
                    start = pl.multiple_of((field * CX + cell_x) * CY + up * TILE, TILE)
                    state_ref[pl.ds(start, TILE), :] = blocks[field][half]
                    prim_ref[pl.ds(start, TILE), :] = density if field == 0 else (
                        pressure if field == 4 else vel[field - 1]
                    )
        return carry

    lax.fori_loop(0, 8, brick, 0)
    x_odd, y_odd = node % 2 == 1, dev % 2 == 1
    x_last, y_last = (CX - 3) * CY, CY - 3
    for odd_x, odd_y, x_ref, y_ref in (
        (x_odd, y_odd, x_first_ref, y_first_ref),
        (~x_odd, ~y_odd, x_second_ref, y_second_ref),
    ):
        x_start = pl.multiple_of(jnp.where(odd_x, 0, x_last), TILE)
        y_start = jnp.where(odd_y, 0, y_last)
        for field in range(FIELDS):
            x_ref[pl.ds(field * 96, 96), :] = prim_ref[pl.ds(field * CX * CY + x_start, 96), :]
            for layer in range(3):
                for block in range(2):
                    start = (field * CX + block * 8) * CY + layer
                    rows = pl.ds((field * 3 + layer) * CX + block * 8, 8)
                    y_ref[rows, :] = prim_ref[pl.ds(start + y_start, 8, stride=CY), :]


def unpack(*operands):
    grid_rows = jax.ShapeDtypeStruct((ROWS, CZ), jnp.float32)
    x_side = jax.ShapeDtypeStruct((FIELDS * 3 * CY, CZ), jnp.float32)
    y_side = jax.ShapeDtypeStruct((FIELDS * 3 * CX, CZ), jnp.float32)
    return call(
        unpack_kernel,
        "unpack",
        (grid_rows, grid_rows, x_side, x_side, y_side, y_side),
        [VMEM] * len(operands),
        scratch_shapes=[pltpu.VMEM((FIELDS, TILES, CELLS), jnp.float32)],
    )(*operands)


def median_zero(first_value, second_value):
    return jnp.maximum(
        jnp.minimum(first_value, 0.0), jnp.minimum(jnp.maximum(first_value, 0.0), second_value)
    )


def interface(prev, here, after, far):
    value = 7.0 / 12.0 * (here + after) - 1.0 / 12.0 * (prev + far)
    return jnp.minimum(jnp.maximum(value, jnp.minimum(here, after)), jnp.maximum(here, after))


def edges(centre, below, above):
    low, high = below - centre, above - centre
    return centre + median_zero(low, -2.0 * high), centre + median_zero(high, -2.0 * low)


def face_flux(left, right, normal):
    def speeds(side):
        scaled = 1.4 * side[4]
        sound = scaled * lax.rsqrt(scaled * side[0])
        return side[normal] - sound, side[normal] + sound

    left_low, left_high = speeds(left)
    right_low, right_high = speeds(right)
    slowest = jnp.minimum(jnp.minimum(left_low, right_low), 0.0)
    fastest = jnp.maximum(jnp.maximum(left_high, right_high), 0.0)
    inverse = 1.0 / (fastest - slowest)
    share_left = fastest * inverse
    share_right = -slowest * inverse
    spread = slowest * share_left
    rate_left = share_left * left[normal] - spread
    rate_right = share_right * right[normal] + spread
    mass_left, mass_right = rate_left * left[0], rate_right * right[0]
    push_left, push_right = share_left * left[4], share_right * right[4]
    flux = [mass_left + mass_right]
    for axis in range(1, 4):
        value = mass_left * left[axis] + mass_right * right[axis]
        if axis == normal:
            value = value + (push_left + push_right)
        flux.append(value)

    def carried(side, rate, mass, push):
        speed_square = side[1] * side[1] + side[2] * side[2] + side[3] * side[3]
        return 2.5 * (rate * side[4]) + 0.5 * (mass * speed_square) + push * side[normal]

    flux.append(
        carried(left, rate_left, mass_left, push_left) + carried(right, rate_right, mass_right, push_right)
    )
    return flux


def sweep(load, count, normal, emit):
    every = range(FIELDS)
    cells = {cell: load(cell) for cell in (-3, -2, -1, 0)}
    below = [interface(cells[-3][f], cells[-2][f], cells[-1][f], cells[0][f]) for f in every]
    left = flux_below = None
    for cell in range(-1, count + 1):
        cells[cell + 2] = load(cell + 2)
        above = [
            interface(cells[cell - 1][f], cells[cell][f], cells[cell + 1][f], cells[cell + 2][f]) for f in every
        ]
        pairs = [edges(cells[cell][f], below[f], above[f]) for f in every]
        if left is not None:
            flux = face_flux(left, [pair[0] for pair in pairs], normal)
            if flux_below is not None:
                emit(cell - 1, [flux[f] - flux_below[f] for f in every])
            flux_below = flux
        left = [pair[1] for pair in pairs]
        below = above


def z_kernel(state_ref, prim_ref, out_ref):
    def rolled(value, shift):
        return pltpu.roll(value, shift % CZ, 1)

    def step(cell_x, carry):
        for up in range(CY // 8):
            starts = [
                pl.multiple_of((f * CX + cell_x) * CY + up * 8, 8) for f in range(FIELDS)
            ]
            here = [prim_ref[pl.ds(start, 8), :] for start in starts]
            lows, highs = [], []
            for value in here:
                after = rolled(value, -1)
                above = interface(rolled(value, 1), value, after, rolled(after, -1))
                low, high = edges(value, rolled(above, 1), above)
                lows.append(rolled(low, -1))
                highs.append(high)
            flux = face_flux(highs, lows, 3)
            for f in range(FIELDS):
                change = flux[f] - rolled(flux[f], 1)
                out_ref[pl.ds(starts[f], 8), :] = state_ref[pl.ds(starts[f], 8), :] - 0.1 * change
        return carry

    lax.fori_loop(0, CX, step, 0, unroll=2)


def side(first_ref, second_ref, odd, before, rows):
    first, second = first_ref[rows, :], second_ref[rows, :]
    return jnp.where(odd, first, second) if before else jnp.where(odd, second, first)


def y_kernel(prim_ref, first_ref, second_ref, change_ref):
    odd = lax.axis_index("dev") % 2 == 1

    def step(block, carry):
        def load(cell):
            if cell < 0 or cell >= CY:
                layer = cell + 3 if cell < 0 else cell - CY
                rows = [pl.ds(pl.multiple_of((f * 3 + layer) * CX + block * 8, 8), 8) for f in range(FIELDS)]
                return [side(first_ref, second_ref, odd, cell < 0, row) for row in rows]
            return [prim_ref[pl.ds((f * CX + block * 8) * CY + cell, 8, stride=CY), :] for f in range(FIELDS)]

        def emit(cell, change):
            for f in range(FIELDS):
                rows = pl.ds(pl.multiple_of((f * CY + cell) * CX + block * 8, 8), 8)
                change_ref[rows, :] = change[f]

        sweep(load, CY, 2, emit)
        return carry

    lax.fori_loop(0, CX // 8, step, 0)


def x_kernel(before_ref, prim_ref, change_ref, first_ref, second_ref, out_ref):
    odd = lax.axis_index("node") % 2 == 1

    def step(block, carry):
        def load(cell):
            if cell < 0 or cell >= CX:
                layer = cell + 3 if cell < 0 else cell - CX
                rows = [pl.ds(pl.multiple_of((f * 3 + layer) * CY + block * 8, 8), 8) for f in range(FIELDS)]
                return [side(first_ref, second_ref, odd, cell < 0, row) for row in rows]
            return [
                prim_ref[pl.ds(pl.multiple_of((f * CX + cell) * CY + block * 8, 8), 8), :] for f in range(FIELDS)
            ]

        def emit(cell, change):
            for f in range(FIELDS):
                rows = pl.ds(pl.multiple_of((f * CX + cell) * CY + block * 8, 8), 8)
                other = change_ref[pl.ds((f * CY + block * 8) * CX + cell, 8, stride=CX), :]
                out_ref[rows, :] = before_ref[rows, :] - 0.1 * (change[f] + other)

        sweep(load, CX, 1, emit)
        return carry

    lax.fori_loop(0, CY // 8, step, 0)


def stage(kernel, name, *operands):
    return call(
        kernel,
        name,
        jax.ShapeDtypeStruct((ROWS, CZ), jnp.float32),
        [VMEM] * len(operands),
        cost_estimate=pl.CostEstimate(flops=20_000_000, bytes_accessed=4_000_000, transcendentals=200_000),
    )(*operands)


def shifted(value, axes, count, target):
    pairs = [(i, target(i)) for i in range(count)]
    return lax.ppermute(value, axes, [pair for pair in pairs if pair[1] >= 0])


def hop(device, step):
    return device + 8 * step if 0 <= device // 8 + step < 16 else -1


def next_node(device):
    other = hop(device, 1 if device % 8 >= 4 else -1)
    return other if other >= 0 else device ^ 4


def onward_node(device):
    dev = device % 8
    return device if 2 <= dev < 6 else hop(device, 1 if dev < 2 else -1)


def masked(value, mask):
    return shifted(value, AXES, 128, lambda device: device ^ mask)


def body(old_state, old_tile_pos):
    pos = old_tile_pos.reshape(1, TILES)
    old = old_state.transpose(1, 0, 2)
    two, three, six, seven, relay = pack_early(pos, old)
    relay = shifted(relay, AXES, 128, next_node)
    six, seven, two, three = masked(six, 6), masked(seven, 7), masked(two, 2), masked(three, 3)
    one, four, five, far, onward = pack_late(pos, old, relay, six, seven)
    onward = shifted(onward, AXES, 128, onward_node)
    four, five, one, far = masked(four, 4), masked(five, 5), masked(one, 1), masked(far, 64)
    state, prim, x_first, x_second, y_first, y_second = unpack(
        pos, old, one, two, three, four, five, far, onward
    )
    x_first = shifted(x_first, "node", 16, lambda i: i ^ 1)
    x_second = shifted(x_second, "node", 16, lambda i: (i + 1) % 16 if i % 2 else (i - 1) % 16)
    y_first = shifted(y_first, "dev", 8, lambda i: i ^ 1)
    y_second = shifted(y_second, "dev", 8, lambda i: (i + 1) % 8 if i % 2 else (i - 1) % 8)
    result = stage(z_kernel, "flux_third", state, prim)
    change = stage(y_kernel, "flux_second", prim, y_first, y_second)
    result = stage(x_kernel, "flux_first", result, prim, change, x_first, x_second)
    return result.reshape(FIELDS, CX, CY, CZ)


def solution(mesh):
    in_specs = (P(AXES, None, None), P(AXES))
    out_specs = P(None, "node", "dev", None)
    return jax.shard_map(body, mesh=mesh, in_specs=in_specs, out_specs=out_specs, check_vma=False)
```

```python
import jax
import jax.numpy as jnp
from jax import lax
from jax.experimental import pallas as pl
from jax.experimental.pallas import tpu as pltpu
from jax.sharding import PartitionSpec as P

CX = 16
CY = 32
CZ = 128
FIELDS = 5
TILE = 8
MOVE = 8
TILES = 128
CELLS = 512
PARTS = CELLS // CZ
PLANES = FIELDS * PARTS + 1
ROWS = FIELDS * CX * CY
VMEM_LIMIT = 48 * 1024 * 1024

EARLY_RELAY = 4 * MOVE
EARLY_ROWS = 6 * MOVE
LATE_ROWS = 4 * MOVE
ARRIVED = 9 * MOVE

AXES = ("node", "dev")


def iota(shape, dim):
    return lax.broadcasted_iota(jnp.int32, shape, dim)


def split3(value):
    high = value.astype(jnp.bfloat16)
    rest = value - high.astype(jnp.float32)
    mid = rest.astype(jnp.bfloat16)
    low = (rest - mid.astype(jnp.float32)).astype(jnp.bfloat16)
    return high, mid, low


def added(terms):
    total = None
    for term in terms:
        total = term if total is None else total + term
    return total


def pick(choice, values):
    return added(
        jnp.dot(choice, part, preferred_element_type=jnp.float32) for part in reversed(split3(values))
    )


def weighted(values, weights):
    return added(
        jnp.dot(part, weights, preferred_element_type=jnp.float32) for part in reversed(split3(values))
    )


def place():
    return lax.axis_index("node"), lax.axis_index("dev")


def targets(pos):
    square = (TILES, TILES)
    by_lane = jnp.broadcast_to(pos // TILES, square)
    by_row = by_lane.T
    earlier = (by_lane == by_row) & (iota(square, 0) < iota(square, 1))
    rank = jnp.sum(earlier.astype(jnp.int32), axis=0, keepdims=True)
    return pos // TILES, pos % TILES, rank


def packed(target, local, rows, old_ref, put):
    shape = (rows, TILES)
    chosen = iota(shape, 0) == jnp.broadcast_to(target, shape)
    code = jnp.sum(
        jnp.where(chosen, jnp.broadcast_to(local + 1, shape), 0).astype(jnp.float32), axis=1, keepdims=True
    )
    put(PLANES - 1, jnp.broadcast_to(code, shape))
    choice = chosen.astype(jnp.float32).astype(jnp.bfloat16)
    for field in range(FIELDS):
        values = pick(choice, old_ref[field])
        for part in range(PARTS):
            put(field * PARTS + part, values[:, part * CZ : (part + 1) * CZ])


def pack_early_kernel(pos_ref, old_ref, two_ref, three_ref, six_ref, seven_ref, relay_ref):
    node, dev = place()
    owner, local, rank = targets(pos_ref[...])
    mask = (owner % 8) ^ dev
    outer, low = mask >= 4, mask % 4
    here = owner // 8 == node
    by_mask = (mask // 4 * 2 + mask % 2) * MOVE + rank
    relayed = EARLY_RELAY + mask % 2 * MOVE + rank
    target = jnp.where(low >= 2, by_mask, jnp.where(outer & ~here, relayed, -1))
    target = jnp.where(owner // 8 == node ^ 8, -1, target)

    def put(plane, value):
        for block, ref in enumerate((two_ref, three_ref, six_ref, seven_ref)):
            ref[plane] = value[block * MOVE : (block + 1) * MOVE]
        for block in range(2):
            first = EARLY_RELAY + block * MOVE
            relay_ref[block, plane] = value[first : first + MOVE]

    packed(target, local, EARLY_ROWS, old_ref, put)


def pack_late_kernel(
    pos_ref, old_ref, relay_ref, six_ref, seven_ref, one_ref, four_ref, five_ref, far_ref, on_ref
):
    node, dev = place()
    owner, local, rank = targets(pos_ref[...])
    mask = (owner % 8) ^ dev
    inside = jnp.where((mask == 1) | (mask == 4) | (mask == 5), (mask // 4 + mask % 2) * MOVE, -TILES)
    inside = jnp.where(mask == 1, 0, inside)
    target = jnp.where(owner // 8 == node, inside, jnp.where(owner // 8 == node ^ 8, 3 * MOVE, -TILES)) + rank

    def put(plane, value):
        one_ref[plane] = value[:MOVE]
        four_ref[0, plane] = value[MOVE : 2 * MOVE]
        four_ref[1, plane] = relay_ref[0, plane]
        five_ref[plane] = value[2 * MOVE : 3 * MOVE] + relay_ref[1, plane]
        far_ref[plane] = value[3 * MOVE :]
        on_ref[0, plane] = six_ref[plane]
        on_ref[1, plane] = seven_ref[plane]

    packed(target, local, LATE_ROWS, old_ref, put)


VMEM = pl.BlockSpec(memory_space=pltpu.VMEM)
BUFFER = jax.ShapeDtypeStruct((PLANES, MOVE, CZ), jnp.float32)


def buffers(count):
    return jax.ShapeDtypeStruct((count,) + BUFFER.shape, jnp.float32)


def call(kernel, name, out_shape, in_specs, **more):
    return pl.pallas_call(
        kernel,
        out_shape=out_shape,
        in_specs=in_specs,
        out_specs=jax.tree.map(lambda _: VMEM, out_shape),
        compiler_params=pltpu.CompilerParams(vmem_limit_bytes=VMEM_LIMIT),
        name=name,
        **more,
    )


def pack_early(pos, old):
    return call(pack_early_kernel, "pack_early", (BUFFER,) * 4 + (buffers(2),), [VMEM, VMEM])(pos, old)


def pack_late(pos, old, relay, six, seven):
    return call(
        pack_late_kernel, "pack_late", (BUFFER, buffers(2), BUFFER, BUFFER, buffers(2)), [VMEM] * 5
    )(pos, old, relay, six, seven)


def grains(first, second, half_low, row_pick, lane_picks):
    first = pltpu.roll(first, 0, 1, stride=TILE, stride_axis=0)
    second = pltpu.roll(second, 64, 1, stride=TILE, stride_axis=0)
    result = []
    for half in range(2):
        mixed = jnp.where(half_low, first, second) if half == 0 else jnp.where(half_low, second, first)
        mixed = jnp.take_along_axis(mixed, row_pick, axis=0)
        result.append(jnp.take_along_axis(mixed, lane_picks[half], axis=1))
    return result


def unpack_kernel(
    pos_ref, old_ref, one_ref, two_ref, three_ref, four_ref, five_ref, far_ref, on_ref,
    state_ref, prim_ref, x_first_ref, x_second_ref, y_first_ref, y_second_ref, tiles_ref,
):
    node, dev = place()
    pos = pos_ref[...]
    square = (TILES, TILES)
    kept = jnp.where(pos // TILES == node * 8 + dev, pos % TILES, -1)
    kept_choice = jnp.broadcast_to(kept, square) == iota(square, 0)

    def arrived(plane):
        blocks = [ref[plane] for ref in (one_ref, two_ref, three_ref, five_ref, far_ref)]
        blocks += [four_ref[0, plane], four_ref[1, plane]]
        blocks += [on_ref[0, plane], on_ref[1, plane]]
        return jnp.concatenate(blocks, axis=0)

    code = jnp.concatenate([arrived(PLANES - 1), jnp.zeros((TILES - ARRIVED, CZ), jnp.float32)], axis=0)
    code = code.T.astype(jnp.int32)
    new_choice = code == iota(square, 0) + 1
    choice = jnp.concatenate([kept_choice, new_choice], axis=1).astype(jnp.float32).astype(jnp.bfloat16)
    blank = jnp.zeros((TILES - ARRIVED, CELLS), jnp.float32)
    for field in range(FIELDS):
        moved = jnp.concatenate([arrived(field * PARTS + part) for part in range(PARTS)], axis=1)
        tiles_ref[field] = pick(choice, jnp.concatenate([old_ref[field], moved, blank], axis=0))

    row = iota((TILE, CZ), 0)
    grain = iota((TILE, CZ), 1) // TILE
    half_low = (grain - row) % 16 < 8
    row_pick = (grain - row) % 8
    lane = iota((TILE, CZ), 1)
    lane_picks = [(lane + TILE * row + 64 * half) % CZ for half in range(2)]

    def brick(index, carry):
        across, up = index // 4, index % 4
        for part in range(PARTS):
            blocks = []
            for field in range(FIELDS):
                lanes = slice(part * CZ, (part + 1) * CZ)
                first = tiles_ref[field, pl.ds(pl.multiple_of(index * 16, 16), 8), lanes]
                second = tiles_ref[field, pl.ds(pl.multiple_of(index * 16 + 8, 8), 8), lanes]
                blocks.append(grains(first, second, half_low, row_pick, lane_picks))
            for half in range(2):
                density, mom_x, mom_y, mom_z, energy = [blocks[field][half] for field in range(FIELDS)]
                inverse = 1.0 / density
                vel = [mom_x * inverse, mom_y * inverse, mom_z * inverse]
                square_sum = vel[0] * vel[0] + vel[1] * vel[1] + vel[2] * vel[2]
                pressure = (1.4 - 1.0) * (energy - 0.5 * density * square_sum)
                cell_x = across * TILE + part * 2 + half
                for field in range(FIELDS):
                    start = pl.multiple_of((field * CX + cell_x) * CY + up * TILE, TILE)
                    state_ref[pl.ds(start, TILE), :] = blocks[field][half]
                    prim_ref[pl.ds(start, TILE), :] = density if field == 0 else (
                        pressure if field == 4 else vel[field - 1]
                    )
        return carry

    lax.fori_loop(0, 8, brick, 0)
    x_odd, y_odd = node % 2 == 1, dev % 2 == 1
    x_last, y_last = (CX - 3) * CY, CY - 3
    for odd_x, odd_y, x_ref, y_ref in (
        (x_odd, y_odd, x_first_ref, y_first_ref),
        (~x_odd, ~y_odd, x_second_ref, y_second_ref),
    ):
        x_start = pl.multiple_of(jnp.where(odd_x, 0, x_last), TILE)
        y_start = jnp.where(odd_y, 0, y_last)
        for field in range(FIELDS):
            x_ref[pl.ds(field * 96, 96), :] = prim_ref[pl.ds(field * CX * CY + x_start, 96), :]
            for layer in range(3):
                for block in range(2):
                    start = (field * CX + block * 8) * CY + layer
                    rows = pl.ds((field * 3 + layer) * CX + block * 8, 8)
                    y_ref[rows, :] = prim_ref[pl.ds(start + y_start, 8, stride=CY), :]


def unpack(*operands):
    grid_rows = jax.ShapeDtypeStruct((ROWS, CZ), jnp.float32)
    x_side = jax.ShapeDtypeStruct((FIELDS * 3 * CY, CZ), jnp.float32)
    y_side = jax.ShapeDtypeStruct((FIELDS * 3 * CX, CZ), jnp.float32)
    return call(
        unpack_kernel,
        "unpack",
        (grid_rows, grid_rows, x_side, x_side, y_side, y_side),
        [VMEM] * len(operands),
        scratch_shapes=[pltpu.VMEM((FIELDS, TILES, CELLS), jnp.float32)],
    )(*operands)


def median_zero(first_value, second_value):
    return jnp.maximum(
        jnp.minimum(first_value, 0.0), jnp.minimum(jnp.maximum(first_value, 0.0), second_value)
    )


def interface(prev, here, after, far):
    value = 7.0 / 12.0 * (here + after) - 1.0 / 12.0 * (prev + far)
    return jnp.minimum(jnp.maximum(value, jnp.minimum(here, after)), jnp.maximum(here, after))


def edges(centre, below, above):
    low, high = below - centre, above - centre
    return centre + median_zero(low, -2.0 * high), centre + median_zero(high, -2.0 * low)


def face_flux(left, right, normal):
    def speeds(side):
        scaled = 1.4 * side[4]
        sound = scaled * lax.rsqrt(scaled * side[0])
        return side[normal] - sound, side[normal] + sound

    left_low, left_high = speeds(left)
    right_low, right_high = speeds(right)
    slowest = jnp.minimum(jnp.minimum(left_low, right_low), 0.0)
    fastest = jnp.maximum(jnp.maximum(left_high, right_high), 0.0)
    inverse = 1.0 / (fastest - slowest)
    share_left = fastest * inverse
    share_right = -slowest * inverse
    spread = slowest * share_left
    rate_left = share_left * left[normal] - spread
    rate_right = share_right * right[normal] + spread
    mass_left, mass_right = rate_left * left[0], rate_right * right[0]
    push_left, push_right = share_left * left[4], share_right * right[4]
    flux = [mass_left + mass_right]
    for axis in range(1, 4):
        value = mass_left * left[axis] + mass_right * right[axis]
        if axis == normal:
            value = value + (push_left + push_right)
        flux.append(value)

    def carried(side, rate, mass, push):
        speed_square = side[1] * side[1] + side[2] * side[2] + side[3] * side[3]
        return 2.5 * (rate * side[4]) + 0.5 * (mass * speed_square) + push * side[normal]

    flux.append(
        carried(left, rate_left, mass_left, push_left) + carried(right, rate_right, mass_right, push_right)
    )
    return flux


def sweep(load, first, last, normal, emit):
    every = range(FIELDS)
    cells = {cell: load(cell) for cell in range(first - 3, first + 1)}
    below = [interface(*[cells[cell][f] for cell in range(first - 3, first + 1)]) for f in every]
    left = flux_below = None
    for cell in range(first - 1, last + 2):
        cells[cell + 2] = load(cell + 2)
        above = [
            interface(cells[cell - 1][f], cells[cell][f], cells[cell + 1][f], cells[cell + 2][f]) for f in every
        ]
        pairs = [edges(cells[cell][f], below[f], above[f]) for f in every]
        if left is not None:
            flux = face_flux(left, [pair[0] for pair in pairs], normal)
            if flux_below is not None:
                emit(cell - 1, [flux[f] - flux_below[f] for f in every])
            flux_below = flux
        left = [pair[1] for pair in pairs]
        below = above


def block_rows(f, cell, block):
    return pl.ds(pl.multiple_of((f * CX + cell) * CY + block * 8, 8), 8)


def inner_kernel(state_ref, prim_ref, out_ref):
    def rolled(value, shift):
        return pltpu.roll(value, shift % CZ, 1)

    ahead = (iota((CZ, CZ), 0) - iota((CZ, CZ), 1)) % CZ
    outer = jnp.where((ahead == CZ - 1) | (ahead == 2), -1.0, 0.0)
    weights = jnp.where(ahead <= 1, 7.0, outer).astype(jnp.bfloat16)
    lows, highs = [], []
    for f in range(FIELDS):
        value = prim_ref[pl.ds(f * CX * CY, CX * CY), :]
        after = rolled(value, -1)
        mean = weighted(value, weights) * (1.0 / 12.0)
        above = jnp.minimum(jnp.maximum(mean, jnp.minimum(value, after)), jnp.maximum(value, after))
        low, high = edges(value, rolled(above, 1), above)
        lows.append(rolled(low, -1))
        highs.append(high)
    flux = face_flux(highs, lows, 3)
    for f in range(FIELDS):
        rows = pl.ds(f * CX * CY, CX * CY)
        out_ref[rows, :] = state_ref[rows, :] - 0.1 * (flux[f] - rolled(flux[f], 1))

    def step(block, carry):
        def load(cell):
            return [prim_ref[block_rows(f, cell, block), :] for f in range(FIELDS)]

        def emit(cell, change):
            for f in range(FIELDS):
                rows = block_rows(f, cell, block)
                out_ref[rows, :] = out_ref[rows, :] - 0.1 * change[f]

        sweep(load, 3, CX - 4, 1, emit)
        return carry

    lax.fori_loop(0, CY // 8, step, 0)


def side(first_ref, second_ref, odd, before, rows):
    first, second = first_ref[rows, :], second_ref[rows, :]
    return jnp.where(odd, first, second) if before else jnp.where(odd, second, first)


def y_kernel(prim_ref, first_ref, second_ref, change_ref):
    odd = lax.axis_index("dev") % 2 == 1

    def step(block, carry):
        def load(cell):
            if cell < 0 or cell >= CY:
                layer = cell + 3 if cell < 0 else cell - CY
                rows = [pl.ds(pl.multiple_of((f * 3 + layer) * CX + block * 8, 8), 8) for f in range(FIELDS)]
                return [side(first_ref, second_ref, odd, cell < 0, row) for row in rows]
            return [prim_ref[pl.ds((f * CX + block * 8) * CY + cell, 8, stride=CY), :] for f in range(FIELDS)]

        def emit(cell, change):
            for f in range(FIELDS):
                rows = pl.ds(pl.multiple_of((f * CY + cell) * CX + block * 8, 8), 8)
                change_ref[rows, :] = change[f]

        sweep(load, 0, CY - 1, 2, emit)
        return carry

    lax.fori_loop(0, CX // 8, step, 0)


def x_kernel(before_ref, prim_ref, change_ref, first_ref, second_ref, out_hbm, out_ref, sems):
    odd = lax.axis_index("node") % 2 == 1

    def leaving(block, field):
        part = (field, slice(None), pl.ds(pl.multiple_of(block * 8, 8), 8))
        return pltpu.make_async_copy(out_ref.at[part], out_hbm.at[part], sems.at[block, field])

    def step(block, carry):
        def load(cell):
            if cell < 0 or cell >= CX:
                layer = cell + 3 if cell < 0 else cell - CX
                rows = [pl.ds(pl.multiple_of((f * 3 + layer) * CY + block * 8, 8), 8) for f in range(FIELDS)]
                return [side(first_ref, second_ref, odd, cell < 0, row) for row in rows]
            return [prim_ref[block_rows(f, cell, block), :] for f in range(FIELDS)]

        def emit(cell, change=None):
            for f in range(FIELDS):
                total = change_ref[pl.ds((f * CY + block * 8) * CX + cell, 8, stride=CX), :]
                if change is not None:
                    total = total + change[f]
                value = before_ref[block_rows(f, cell, block), :] - 0.1 * total
                out_ref[f, cell, pl.ds(pl.multiple_of(block * 8, 8), 8), :] = value

        sweep(load, 0, 2, 1, emit)
        for cell in range(3, CX - 3):
            emit(cell)
        sweep(load, CX - 3, CX - 1, 1, emit)
        for field in range(FIELDS):
            leaving(block, field).start()
        return carry

    lax.fori_loop(0, CY // 8, step, 0)
    for block in range(CY // 8):
        for field in range(FIELDS):
            leaving(block, field).wait()


def stage(kernel, name, *operands):
    return call(
        kernel,
        name,
        jax.ShapeDtypeStruct((ROWS, CZ), jnp.float32),
        [VMEM] * len(operands),
        cost_estimate=pl.CostEstimate(flops=20_000_000, bytes_accessed=4_000_000, transcendentals=200_000),
    )(*operands)


def finish(*operands):
    shape = (FIELDS, CX, CY, CZ)
    return pl.pallas_call(
        x_kernel,
        out_shape=jax.ShapeDtypeStruct(shape, jnp.float32),
        in_specs=[VMEM] * len(operands),
        out_specs=pl.BlockSpec(memory_space=pl.ANY),
        scratch_shapes=[pltpu.VMEM(shape, jnp.float32), pltpu.SemaphoreType.DMA((CY // 8, FIELDS))],
        compiler_params=pltpu.CompilerParams(vmem_limit_bytes=VMEM_LIMIT),
        name="flux_first",
    )(*operands)


def shifted(value, axes, count, target):
    pairs = [(i, target(i)) for i in range(count)]
    return lax.ppermute(value, axes, [pair for pair in pairs if pair[1] >= 0])


def hop(device, step):
    return device + 8 * step if 0 <= device // 8 + step < 16 else -1


def next_node(device):
    other = hop(device, 1 if device % 8 >= 4 else -1)
    return other if other >= 0 else device ^ 4


def onward_node(device):
    dev = device % 8
    return device if 2 <= dev < 6 else hop(device, 1 if dev < 2 else -1)


def masked(value, mask):
    return shifted(value, AXES, 128, lambda device: device ^ mask)


def body(old_state, old_tile_pos):
    pos = old_tile_pos.reshape(1, TILES)
    old = old_state.transpose(1, 0, 2)
    two, three, six, seven, relay = pack_early(pos, old)
    relay = shifted(relay, AXES, 128, next_node)
    six, seven, two, three = masked(six, 6), masked(seven, 7), masked(two, 2), masked(three, 3)
    one, four, five, far, onward = pack_late(pos, old, relay, six, seven)
    onward = shifted(onward, AXES, 128, onward_node)
    four, five, one, far = masked(four, 4), masked(five, 5), masked(one, 1), masked(far, 64)
    state, prim, x_first, x_second, y_first, y_second = unpack(
        pos, old, one, two, three, four, five, far, onward
    )
    x_first = shifted(x_first, "node", 16, lambda i: i ^ 1)
    x_second = shifted(x_second, "node", 16, lambda i: (i + 1) % 16 if i % 2 else (i - 1) % 16)
    y_first = shifted(y_first, "dev", 8, lambda i: i ^ 1)
    y_second = shifted(y_second, "dev", 8, lambda i: (i + 1) % 8 if i % 2 else (i - 1) % 8)
    result = stage(inner_kernel, "flux_inner", state, prim)
    change = stage(y_kernel, "flux_second", prim, y_first, y_second)
    return finish(result, prim, change, x_first, x_second)


def solution(mesh):
    in_specs = (P(AXES, None, None), P(AXES))
    out_specs = P(None, "node", "dev", None)
    return jax.shard_map(body, mesh=mesh, in_specs=in_specs, out_specs=out_specs, check_vma=False)
```

```python
import jax
import jax.numpy as jnp
from jax import lax
from jax.experimental import pallas as pl
from jax.experimental.pallas import tpu as pltpu
from jax.sharding import PartitionSpec as P

CX = 16
CY = 32
CZ = 128
FIELDS = 5
TILE = 8
MOVE = 8
TILES = 128
CELLS = 512
PARTS = CELLS // CZ
PLANES = FIELDS * PARTS + 1
ROWS = FIELDS * CX * CY
VMEM_LIMIT = 48 * 1024 * 1024

EARLY_RELAY = 4 * MOVE
EARLY_ROWS = 6 * MOVE
LATE_ROWS = 4 * MOVE
ARRIVED = 9 * MOVE

AXES = ("node", "dev")


def iota(shape, dim):
    return lax.broadcasted_iota(jnp.int32, shape, dim)


def split3(value):
    high = value.astype(jnp.bfloat16)
    rest = value - high.astype(jnp.float32)
    mid = rest.astype(jnp.bfloat16)
    low = (rest - mid.astype(jnp.float32)).astype(jnp.bfloat16)
    return high, mid, low


def added(terms):
    total = None
    for term in terms:
        total = term if total is None else total + term
    return total


def pick(choice, values):
    return added(
        jnp.dot(choice, part, preferred_element_type=jnp.float32) for part in reversed(split3(values))
    )


def weighted(values, weights):
    return added(
        jnp.dot(part, weights, preferred_element_type=jnp.float32) for part in reversed(split3(values))
    )


def place():
    return lax.axis_index("node"), lax.axis_index("dev")


def targets(pos):
    square = (TILES, TILES)
    by_lane = jnp.broadcast_to(pos // TILES, square)
    by_row = by_lane.T
    earlier = (by_lane == by_row) & (iota(square, 0) < iota(square, 1))
    rank = jnp.sum(earlier.astype(jnp.int32), axis=0, keepdims=True)
    return pos // TILES, pos % TILES, rank


def packed(target, local, rows, old_ref, put):
    shape = (rows, TILES)
    chosen = iota(shape, 0) == jnp.broadcast_to(target, shape)
    code = jnp.sum(
        jnp.where(chosen, jnp.broadcast_to(local + 1, shape), 0).astype(jnp.float32), axis=1, keepdims=True
    )
    put(PLANES - 1, jnp.broadcast_to(code, shape))
    choice = chosen.astype(jnp.float32).astype(jnp.bfloat16)
    for field in range(FIELDS):
        values = pick(choice, old_ref[field])
        for part in range(PARTS):
            put(field * PARTS + part, values[:, part * CZ : (part + 1) * CZ])


def pack_early_kernel(pos_ref, old_ref, two_ref, three_ref, six_ref, seven_ref, relay_ref):
    node, dev = place()
    owner, local, rank = targets(pos_ref[...])
    mask = (owner % 8) ^ dev
    outer, low = mask >= 4, mask % 4
    here = owner // 8 == node
    by_mask = (mask // 4 * 2 + mask % 2) * MOVE + rank
    relayed = EARLY_RELAY + mask % 2 * MOVE + rank
    target = jnp.where(low >= 2, by_mask, jnp.where(outer & ~here, relayed, -1))
    target = jnp.where(owner // 8 == node ^ 8, -1, target)

    def put(plane, value):
        for block, ref in enumerate((two_ref, three_ref, six_ref, seven_ref)):
            ref[plane] = value[block * MOVE : (block + 1) * MOVE]
        for block in range(2):
            first = EARLY_RELAY + block * MOVE
            relay_ref[block, plane] = value[first : first + MOVE]

    packed(target, local, EARLY_ROWS, old_ref, put)


def pack_late_kernel(
    pos_ref, old_ref, relay_ref, six_ref, seven_ref, one_ref, four_ref, five_ref, far_ref, on_ref
):
    node, dev = place()
    owner, local, rank = targets(pos_ref[...])
    mask = (owner % 8) ^ dev
    inside = jnp.where((mask == 1) | (mask == 4) | (mask == 5), (mask // 4 + mask % 2) * MOVE, -TILES)
    inside = jnp.where(mask == 1, 0, inside)
    target = jnp.where(owner // 8 == node, inside, jnp.where(owner // 8 == node ^ 8, 3 * MOVE, -TILES)) + rank

    def put(plane, value):
        one_ref[plane] = value[:MOVE]
        four_ref[0, plane] = value[MOVE : 2 * MOVE]
        four_ref[1, plane] = relay_ref[0, plane]
        five_ref[plane] = value[2 * MOVE : 3 * MOVE] + relay_ref[1, plane]
        far_ref[plane] = value[3 * MOVE :]
        on_ref[0, plane] = six_ref[plane]
        on_ref[1, plane] = seven_ref[plane]

    packed(target, local, LATE_ROWS, old_ref, put)


VMEM = pl.BlockSpec(memory_space=pltpu.VMEM)
BUFFER = jax.ShapeDtypeStruct((PLANES, MOVE, CZ), jnp.float32)


def buffers(count):
    return jax.ShapeDtypeStruct((count,) + BUFFER.shape, jnp.float32)


def call(kernel, name, out_shape, in_specs, **more):
    return pl.pallas_call(
        kernel,
        out_shape=out_shape,
        in_specs=in_specs,
        out_specs=jax.tree.map(lambda _: VMEM, out_shape),
        compiler_params=pltpu.CompilerParams(vmem_limit_bytes=VMEM_LIMIT),
        name=name,
        **more,
    )


def pack_early(pos, old):
    return call(pack_early_kernel, "pack_early", (BUFFER,) * 4 + (buffers(2),), [VMEM, VMEM])(pos, old)


def pack_late(pos, old, relay, six, seven):
    return call(
        pack_late_kernel, "pack_late", (BUFFER, buffers(2), BUFFER, BUFFER, buffers(2)), [VMEM] * 5
    )(pos, old, relay, six, seven)


def grains(first, second, half_low, row_pick, lane_picks):
    first = pltpu.roll(first, 0, 1, stride=TILE, stride_axis=0)
    second = pltpu.roll(second, 64, 1, stride=TILE, stride_axis=0)
    result = []
    for half in range(2):
        mixed = jnp.where(half_low, first, second) if half == 0 else jnp.where(half_low, second, first)
        mixed = jnp.take_along_axis(mixed, row_pick, axis=0)
        result.append(jnp.take_along_axis(mixed, lane_picks[half], axis=1))
    return result


def unpack_kernel(
    pos_ref, old_ref, one_ref, two_ref, three_ref, four_ref, five_ref, far_ref, on_ref,
    state_ref, prim_ref, x_first_ref, x_second_ref, y_first_ref, y_second_ref, tiles_ref,
):
    node, dev = place()
    pos = pos_ref[...]
    square = (TILES, TILES)
    kept = jnp.where(pos // TILES == node * 8 + dev, pos % TILES, -1)
    kept_choice = jnp.broadcast_to(kept, square) == iota(square, 0)

    def arrived(plane):
        blocks = [ref[plane] for ref in (one_ref, two_ref, three_ref, five_ref, far_ref)]
        blocks += [four_ref[0, plane], four_ref[1, plane]]
        blocks += [on_ref[0, plane], on_ref[1, plane]]
        return jnp.concatenate(blocks, axis=0)

    code = jnp.concatenate([arrived(PLANES - 1), jnp.zeros((TILES - ARRIVED, CZ), jnp.float32)], axis=0)
    code = code.T.astype(jnp.int32)
    new_choice = code == iota(square, 0) + 1
    choice = jnp.concatenate([kept_choice, new_choice], axis=1).astype(jnp.float32).astype(jnp.bfloat16)
    blank = jnp.zeros((TILES - ARRIVED, CELLS), jnp.float32)
    for field in range(FIELDS):
        moved = jnp.concatenate([arrived(field * PARTS + part) for part in range(PARTS)], axis=1)
        tiles_ref[field] = pick(choice, jnp.concatenate([old_ref[field], moved, blank], axis=0))

    row = iota((TILE, CZ), 0)
    grain = iota((TILE, CZ), 1) // TILE
    half_low = (grain - row) % 16 < 8
    row_pick = (grain - row) % 8
    lane = iota((TILE, CZ), 1)
    lane_picks = [(lane + TILE * row + 64 * half) % CZ for half in range(2)]

    def brick(index, carry):
        across, up = index // 4, index % 4
        for part in range(PARTS):
            blocks = []
            for field in range(FIELDS):
                lanes = slice(part * CZ, (part + 1) * CZ)
                first = tiles_ref[field, pl.ds(pl.multiple_of(index * 16, 16), 8), lanes]
                second = tiles_ref[field, pl.ds(pl.multiple_of(index * 16 + 8, 8), 8), lanes]
                blocks.append(grains(first, second, half_low, row_pick, lane_picks))
            for half in range(2):
                density, mom_x, mom_y, mom_z, energy = [blocks[field][half] for field in range(FIELDS)]
                inverse = 1.0 / density
                vel = [mom_x * inverse, mom_y * inverse, mom_z * inverse]
                square_sum = vel[0] * vel[0] + vel[1] * vel[1] + vel[2] * vel[2]
                pressure = (1.4 - 1.0) * (energy - 0.5 * density * square_sum)
                cell_x = across * TILE + part * 2 + half
                for field in range(FIELDS):
                    start = pl.multiple_of((field * CX + cell_x) * CY + up * TILE, TILE)
                    state_ref[pl.ds(start, TILE), :] = blocks[field][half]
                    prim_ref[pl.ds(start, TILE), :] = density if field == 0 else (
                        pressure if field == 4 else vel[field - 1]
                    )
        return carry

    lax.fori_loop(0, 8, brick, 0)
    x_odd, y_odd = node % 2 == 1, dev % 2 == 1
    x_last, y_last = (CX - 3) * CY, CY - 3
    for odd_x, odd_y, x_ref, y_ref in (
        (x_odd, y_odd, x_first_ref, y_first_ref),
        (~x_odd, ~y_odd, x_second_ref, y_second_ref),
    ):
        x_start = pl.multiple_of(jnp.where(odd_x, 0, x_last), TILE)
        y_start = jnp.where(odd_y, 0, y_last)
        for field in range(FIELDS):
            x_ref[pl.ds(field * 96, 96), :] = prim_ref[pl.ds(field * CX * CY + x_start, 96), :]
            for layer in range(3):
                for block in range(2):
                    start = (field * CX + block * 8) * CY + layer
                    rows = pl.ds((field * 3 + layer) * CX + block * 8, 8)
                    y_ref[rows, :] = prim_ref[pl.ds(start + y_start, 8, stride=CY), :]


def unpack(*operands):
    grid_rows = jax.ShapeDtypeStruct((ROWS, CZ), jnp.float32)
    x_side = jax.ShapeDtypeStruct((FIELDS * 3 * CY, CZ), jnp.float32)
    y_side = jax.ShapeDtypeStruct((FIELDS * 3 * CX, CZ), jnp.float32)
    return call(
        unpack_kernel,
        "unpack",
        (grid_rows, grid_rows, x_side, x_side, y_side, y_side),
        [VMEM] * len(operands),
        scratch_shapes=[pltpu.VMEM((FIELDS, TILES, CELLS), jnp.float32)],
    )(*operands)


def median_zero(first_value, second_value):
    return jnp.maximum(
        jnp.minimum(first_value, 0.0), jnp.minimum(jnp.maximum(first_value, 0.0), second_value)
    )


def interface(prev, here, after, far):
    value = 7.0 / 12.0 * (here + after) - 1.0 / 12.0 * (prev + far)
    return jnp.minimum(jnp.maximum(value, jnp.minimum(here, after)), jnp.maximum(here, after))


def edges(centre, below, above):
    low, high = below - centre, above - centre
    return centre + median_zero(low, -2.0 * high), centre + median_zero(high, -2.0 * low)


def face_flux(left, right, normal):
    def speeds(side):
        scaled = 1.4 * side[4]
        sound = scaled * lax.rsqrt(scaled * side[0])
        return side[normal] - sound, side[normal] + sound

    left_low, left_high = speeds(left)
    right_low, right_high = speeds(right)
    slowest = jnp.minimum(jnp.minimum(left_low, right_low), 0.0)
    fastest = jnp.maximum(jnp.maximum(left_high, right_high), 0.0)
    inverse = 1.0 / (fastest - slowest)
    share_left = fastest * inverse
    share_right = -slowest * inverse
    spread = slowest * share_left
    rate_left = share_left * left[normal] - spread
    rate_right = share_right * right[normal] + spread
    mass_left, mass_right = rate_left * left[0], rate_right * right[0]
    push_left, push_right = share_left * left[4], share_right * right[4]
    flux = [mass_left + mass_right]
    for axis in range(1, 4):
        value = mass_left * left[axis] + mass_right * right[axis]
        if axis == normal:
            value = value + (push_left + push_right)
        flux.append(value)

    def carried(side, rate, mass, push):
        speed_square = side[1] * side[1] + side[2] * side[2] + side[3] * side[3]
        return 2.5 * (rate * side[4]) + 0.5 * (mass * speed_square) + push * side[normal]

    flux.append(
        carried(left, rate_left, mass_left, push_left) + carried(right, rate_right, mass_right, push_right)
    )
    return flux


def sweep(load, first, last, normal, emit):
    every = range(FIELDS)
    cells = {cell: load(cell) for cell in range(first - 3, first + 1)}
    below = [interface(*[cells[cell][f] for cell in range(first - 3, first + 1)]) for f in every]
    left = flux_below = None
    for cell in range(first - 1, last + 2):
        cells[cell + 2] = load(cell + 2)
        above = [
            interface(cells[cell - 1][f], cells[cell][f], cells[cell + 1][f], cells[cell + 2][f]) for f in every
        ]
        pairs = [edges(cells[cell][f], below[f], above[f]) for f in every]
        if left is not None:
            flux = face_flux(left, [pair[0] for pair in pairs], normal)
            if flux_below is not None:
                emit(cell - 1, [flux[f] - flux_below[f] for f in every])
            flux_below = flux
        left = [pair[1] for pair in pairs]
        below = above


def block_rows(f, cell, block):
    return pl.ds(pl.multiple_of((f * CX + cell) * CY + block * 8, 8), 8)


def inner_kernel(state_ref, prim_ref, out_ref):
    def rolled(value, shift):
        return pltpu.roll(value, shift % CZ, 1)

    ahead = (iota((CZ, CZ), 0) - iota((CZ, CZ), 1)) % CZ
    outer = jnp.where((ahead == CZ - 1) | (ahead == 2), -1.0, 0.0)
    weights = jnp.where(ahead <= 1, 7.0, outer).astype(jnp.bfloat16)
    lows, highs = [], []
    for f in range(FIELDS):
        value = prim_ref[pl.ds(f * CX * CY, CX * CY), :]
        after = rolled(value, -1)
        mean = weighted(value, weights) * (1.0 / 12.0)
        above = jnp.minimum(jnp.maximum(mean, jnp.minimum(value, after)), jnp.maximum(value, after))
        low, high = edges(value, rolled(above, 1), above)
        lows.append(rolled(low, -1))
        highs.append(high)
    flux = face_flux(highs, lows, 3)
    for f in range(FIELDS):
        rows = pl.ds(f * CX * CY, CX * CY)
        out_ref[rows, :] = state_ref[rows, :] - 0.1 * (flux[f] - rolled(flux[f], 1))

    def step(block, carry):
        def load(cell):
            return [prim_ref[block_rows(f, cell, block), :] for f in range(FIELDS)]

        def emit(cell, change):
            for f in range(FIELDS):
                rows = block_rows(f, cell, block)
                out_ref[rows, :] = out_ref[rows, :] - 0.1 * change[f]

        sweep(load, 3, CX - 4, 1, emit)
        return carry

    lax.fori_loop(0, CY // 8, step, 0)


def side(first_ref, second_ref, odd, before, rows):
    first, second = first_ref[rows, :], second_ref[rows, :]
    return jnp.where(odd, first, second) if before else jnp.where(odd, second, first)


def y_kernel(prim_ref, first_ref, second_ref, change_ref):
    odd = lax.axis_index("dev") % 2 == 1

    def step(block, carry):
        def load(cell):
            if cell < 0 or cell >= CY:
                layer = cell + 3 if cell < 0 else cell - CY
                rows = [pl.ds(pl.multiple_of((f * 3 + layer) * CX + block * 8, 8), 8) for f in range(FIELDS)]
                return [side(first_ref, second_ref, odd, cell < 0, row) for row in rows]
            return [prim_ref[pl.ds((f * CX + block * 8) * CY + cell, 8, stride=CY), :] for f in range(FIELDS)]

        def emit(cell, change):
            for f in range(FIELDS):
                rows = pl.ds(pl.multiple_of((f * CY + cell) * CX + block * 8, 8), 8)
                change_ref[rows, :] = change[f]

        sweep(load, 0, CY - 1, 2, emit)
        return carry

    lax.fori_loop(0, CX // 8, step, 0)


def x_kernel(before_ref, prim_ref, change_ref, first_ref, second_ref, out_hbm, out_ref, sems):
    odd = lax.axis_index("node") % 2 == 1

    def leaving(block, field):
        part = (field, slice(None), pl.ds(pl.multiple_of(block * 8, 8), 8))
        return pltpu.make_async_copy(out_ref.at[part], out_hbm.at[part], sems.at[block, field])

    def step(block, carry):
        def load(cell):
            if cell < 0 or cell >= CX:
                layer = cell + 3 if cell < 0 else cell - CX
                rows = [pl.ds(pl.multiple_of((f * 3 + layer) * CY + block * 8, 8), 8) for f in range(FIELDS)]
                return [side(first_ref, second_ref, odd, cell < 0, row) for row in rows]
            return [prim_ref[block_rows(f, cell, block), :] for f in range(FIELDS)]

        def emit(cell, change=None):
            for f in range(FIELDS):
                total = change_ref[pl.ds((f * CY + block * 8) * CX + cell, 8, stride=CX), :]
                if change is not None:
                    total = total + change[f]
                value = before_ref[block_rows(f, cell, block), :] - 0.1 * total
                out_ref[f, cell, pl.ds(pl.multiple_of(block * 8, 8), 8), :] = value

        sweep(load, 0, 2, 1, emit)
        for cell in range(3, CX - 3):
            emit(cell)
        sweep(load, CX - 3, CX - 1, 1, emit)
        for field in range(FIELDS):
            leaving(block, field).start()
        return carry

    lax.fori_loop(0, CY // 8, step, 0)
    for block in range(CY // 8):
        for field in range(FIELDS):
            leaving(block, field).wait()


def stage(kernel, name, *operands):
    return call(
        kernel,
        name,
        jax.ShapeDtypeStruct((ROWS, CZ), jnp.float32),
        [VMEM] * len(operands),
        cost_estimate=pl.CostEstimate(flops=20_000_000, bytes_accessed=4_000_000, transcendentals=200_000),
    )(*operands)


def finish(*operands):
    shape = (FIELDS, CX, CY, CZ)
    return pl.pallas_call(
        x_kernel,
        out_shape=jax.ShapeDtypeStruct(shape, jnp.float32),
        in_specs=[VMEM] * len(operands),
        out_specs=pl.BlockSpec(memory_space=pl.ANY),
        scratch_shapes=[pltpu.VMEM(shape, jnp.float32), pltpu.SemaphoreType.DMA((CY // 8, FIELDS))],
        compiler_params=pltpu.CompilerParams(vmem_limit_bytes=VMEM_LIMIT),
        name="flux_first",
    )(*operands)


def shifted(value, axes, count, target):
    pairs = [(i, target(i)) for i in range(count)]
    return lax.ppermute(value, axes, [pair for pair in pairs if pair[1] >= 0])


def hop(device, step):
    return device + 8 * step if 0 <= device // 8 + step < 16 else -1


def next_node(device):
    other = hop(device, 1 if device % 8 >= 4 else -1)
    return other if other >= 0 else device ^ 6


def onward_node(device):
    dev = device % 8
    return device if 2 <= dev < 6 else hop(device, 1 if dev < 2 else -1)


def masked(value, mask):
    return shifted(value, AXES, 128, lambda device: device ^ mask)


def body(old_state, old_tile_pos):
    pos = old_tile_pos.reshape(1, TILES)
    old = old_state.transpose(1, 0, 2)
    two, three, six, seven, relay = pack_early(pos, old)
    relay = shifted(relay, AXES, 128, next_node)
    six, seven, two, three = masked(six, 6), masked(seven, 7), masked(two, 2), masked(three, 3)
    one, four, five, far, onward = pack_late(pos, old, relay, six, seven)
    onward = shifted(onward, AXES, 128, onward_node)
    four, five, one, far = masked(four, 4), masked(five, 5), masked(one, 1), masked(far, 64)
    state, prim, x_first, x_second, y_first, y_second = unpack(
        pos, old, one, two, three, four, five, far, onward
    )
    x_first = shifted(x_first, "node", 16, lambda i: i ^ 1)
    x_second = shifted(x_second, "node", 16, lambda i: (i + 1) % 16 if i % 2 else (i - 1) % 16)
    y_first = shifted(y_first, "dev", 8, lambda i: i ^ 1)
    y_second = shifted(y_second, "dev", 8, lambda i: (i + 1) % 8 if i % 2 else (i - 1) % 8)
    result = stage(inner_kernel, "flux_inner", state, prim)
    change = stage(y_kernel, "flux_second", prim, y_first, y_second)
    return finish(result, prim, change, x_first, x_second)


def solution(mesh):
    in_specs = (P(AXES, None, None), P(AXES))
    out_specs = P(None, "node", "dev", None)
    return jax.shard_map(body, mesh=mesh, in_specs=in_specs, out_specs=out_specs, check_vma=False)
```

```python
import jax
import jax.numpy as jnp
from jax import lax
from jax.experimental import pallas as pl
from jax.experimental.pallas import tpu as pltpu
from jax.sharding import PartitionSpec as P

CX = 16
CY = 32
CZ = 128
FIELDS = 5
TILE = 8
MOVE = 8
TILES = 128
CELLS = 512
PARTS = CELLS // CZ
PLANES = FIELDS * PARTS + 1
ROWS = FIELDS * CX * CY
VMEM_LIMIT = 48 * 1024 * 1024

EARLY_RELAY = 4 * MOVE
EARLY_ROWS = 6 * MOVE
LATE_ROWS = 4 * MOVE
ARRIVED = 9 * MOVE

AXES = ("node", "dev")


def iota(shape, dim):
    return lax.broadcasted_iota(jnp.int32, shape, dim)


def split3(value):
    high = value.astype(jnp.bfloat16)
    rest = value - high.astype(jnp.float32)
    mid = rest.astype(jnp.bfloat16)
    low = (rest - mid.astype(jnp.float32)).astype(jnp.bfloat16)
    return high, mid, low


def added(terms):
    total = None
    for term in terms:
        total = term if total is None else total + term
    return total


def pick(choice, values):
    return added(
        jnp.dot(choice, part, preferred_element_type=jnp.float32) for part in reversed(split3(values))
    )


def weighted(values, weights):
    return added(
        jnp.dot(part, weights, preferred_element_type=jnp.float32) for part in reversed(split3(values))
    )


def place():
    return lax.axis_index("node"), lax.axis_index("dev")


def targets(pos):
    square = (TILES, TILES)
    by_lane = jnp.broadcast_to(pos // TILES, square)
    by_row = by_lane.T
    earlier = (by_lane == by_row) & (iota(square, 0) < iota(square, 1))
    rank = jnp.sum(earlier.astype(jnp.int32), axis=0, keepdims=True)
    return pos // TILES, pos % TILES, rank


def packed(target, local, rows, old_ref, put):
    shape = (rows, TILES)
    chosen = iota(shape, 0) == jnp.broadcast_to(target, shape)
    code = jnp.sum(
        jnp.where(chosen, jnp.broadcast_to(local + 1, shape), 0).astype(jnp.float32), axis=1, keepdims=True
    )
    put(PLANES - 1, jnp.broadcast_to(code, shape))
    choice = chosen.astype(jnp.float32).astype(jnp.bfloat16)
    for field in range(FIELDS):
        values = pick(choice, old_ref[field])
        for part in range(PARTS):
            put(field * PARTS + part, values[:, part * CZ : (part + 1) * CZ])


def pack_early_kernel(pos_ref, old_ref, two_ref, three_ref, six_ref, seven_ref, relay_ref):
    node, dev = place()
    owner, local, rank = targets(pos_ref[...])
    mask = (owner % 8) ^ dev
    outer, low = mask >= 4, mask % 4
    here = owner // 8 == node
    by_mask = (mask // 4 * 2 + mask % 2) * MOVE + rank
    relayed = EARLY_RELAY + mask % 2 * MOVE + rank
    target = jnp.where(low >= 2, by_mask, jnp.where(outer & ~here, relayed, -1))
    target = jnp.where(owner // 8 == node ^ 8, -1, target)

    def put(plane, value):
        for block, ref in enumerate((two_ref, three_ref, six_ref, seven_ref)):
            ref[plane] = value[block * MOVE : (block + 1) * MOVE]
        for block in range(2):
            first = EARLY_RELAY + block * MOVE
            relay_ref[block, plane] = value[first : first + MOVE]

    packed(target, local, EARLY_ROWS, old_ref, put)


def pack_late_kernel(
    pos_ref, old_ref, relay_ref, six_ref, seven_ref, one_ref, four_ref, five_ref, far_ref, on_ref
):
    node, dev = place()
    owner, local, rank = targets(pos_ref[...])
    mask = (owner % 8) ^ dev
    inside = jnp.where((mask == 1) | (mask == 4) | (mask == 5), (mask // 4 + mask % 2) * MOVE, -TILES)
    inside = jnp.where(mask == 1, 0, inside)
    target = jnp.where(owner // 8 == node, inside, jnp.where(owner // 8 == node ^ 8, 3 * MOVE, -TILES)) + rank

    def put(plane, value):
        one_ref[plane] = value[:MOVE]
        four_ref[0, plane] = value[MOVE : 2 * MOVE]
        four_ref[1, plane] = relay_ref[0, plane]
        five_ref[plane] = value[2 * MOVE : 3 * MOVE] + relay_ref[1, plane]
        far_ref[plane] = value[3 * MOVE :]
        on_ref[0, plane] = six_ref[plane]
        on_ref[1, plane] = seven_ref[plane]

    packed(target, local, LATE_ROWS, old_ref, put)


VMEM = pl.BlockSpec(memory_space=pltpu.VMEM)
BUFFER = jax.ShapeDtypeStruct((PLANES, MOVE, CZ), jnp.float32)


def buffers(count):
    return jax.ShapeDtypeStruct((count,) + BUFFER.shape, jnp.float32)


def call(kernel, name, out_shape, in_specs, **more):
    return pl.pallas_call(
        kernel,
        out_shape=out_shape,
        in_specs=in_specs,
        out_specs=jax.tree.map(lambda _: VMEM, out_shape),
        compiler_params=pltpu.CompilerParams(vmem_limit_bytes=VMEM_LIMIT),
        name=name,
        **more,
    )


def pack_early(pos, old):
    return call(pack_early_kernel, "pack_early", (BUFFER,) * 4 + (buffers(2),), [VMEM, VMEM])(pos, old)


def pack_late(pos, old, relay, six, seven):
    return call(
        pack_late_kernel, "pack_late", (BUFFER, buffers(2), BUFFER, BUFFER, buffers(2)), [VMEM] * 5
    )(pos, old, relay, six, seven)


def grains(first, second, half_low, row_pick, lane_picks):
    first = pltpu.roll(first, 0, 1, stride=TILE, stride_axis=0)
    second = pltpu.roll(second, 64, 1, stride=TILE, stride_axis=0)
    result = []
    for half in range(2):
        mixed = jnp.where(half_low, first, second) if half == 0 else jnp.where(half_low, second, first)
        mixed = jnp.take_along_axis(mixed, row_pick, axis=0)
        result.append(jnp.take_along_axis(mixed, lane_picks[half], axis=1))
    return result


def unpack_kernel(
    pos_ref, old_ref, one_ref, two_ref, three_ref, four_ref, five_ref, far_ref, on_ref,
    state_ref, prim_ref, x_first_ref, x_second_ref, y_first_ref, y_second_ref, tiles_ref,
):
    node, dev = place()
    pos = pos_ref[...]
    square = (TILES, TILES)
    kept = jnp.where(pos // TILES == node * 8 + dev, pos % TILES, -1)
    kept_choice = jnp.broadcast_to(kept, square) == iota(square, 0)

    def arrived(plane):
        blocks = [ref[plane] for ref in (one_ref, two_ref, three_ref, five_ref, far_ref)]
        blocks += [four_ref[0, plane], four_ref[1, plane]]
        blocks += [on_ref[0, plane], on_ref[1, plane]]
        return jnp.concatenate(blocks, axis=0)

    code = jnp.concatenate([arrived(PLANES - 1), jnp.zeros((TILES - ARRIVED, CZ), jnp.float32)], axis=0)
    code = code.T.astype(jnp.int32)
    new_choice = code == iota(square, 0) + 1
    choice = jnp.concatenate([kept_choice, new_choice], axis=1).astype(jnp.float32).astype(jnp.bfloat16)
    blank = jnp.zeros((TILES - ARRIVED, CELLS), jnp.float32)
    for field in range(FIELDS):
        moved = jnp.concatenate([arrived(field * PARTS + part) for part in range(PARTS)], axis=1)
        tiles_ref[field] = pick(choice, jnp.concatenate([old_ref[field], moved, blank], axis=0))

    row = iota((TILE, CZ), 0)
    grain = iota((TILE, CZ), 1) // TILE
    half_low = (grain - row) % 16 < 8
    row_pick = (grain - row) % 8
    lane = iota((TILE, CZ), 1)
    lane_picks = [(lane + TILE * row + 64 * half) % CZ for half in range(2)]

    def brick(index, carry):
        across, up = index // 4, index % 4
        for part in range(PARTS):
            blocks = []
            for field in range(FIELDS):
                lanes = slice(part * CZ, (part + 1) * CZ)
                first = tiles_ref[field, pl.ds(pl.multiple_of(index * 16, 16), 8), lanes]
                second = tiles_ref[field, pl.ds(pl.multiple_of(index * 16 + 8, 8), 8), lanes]
                blocks.append(grains(first, second, half_low, row_pick, lane_picks))
            for half in range(2):
                density, mom_x, mom_y, mom_z, energy = [blocks[field][half] for field in range(FIELDS)]
                inverse = 1.0 / density
                vel = [mom_x * inverse, mom_y * inverse, mom_z * inverse]
                square_sum = vel[0] * vel[0] + vel[1] * vel[1] + vel[2] * vel[2]
                pressure = (1.4 - 1.0) * (energy - 0.5 * density * square_sum)
                cell_x = across * TILE + part * 2 + half
                for field in range(FIELDS):
                    start = pl.multiple_of((field * CX + cell_x) * CY + up * TILE, TILE)
                    state_ref[pl.ds(start, TILE), :] = blocks[field][half]
                    prim_ref[pl.ds(start, TILE), :] = density if field == 0 else (
                        pressure if field == 4 else vel[field - 1]
                    )
        return carry

    lax.fori_loop(0, 8, brick, 0)
    x_odd, y_odd = node % 2 == 1, dev % 2 == 1
    x_last, y_last = (CX - 3) * CY, CY - 3
    for odd_x, odd_y, x_ref, y_ref in (
        (x_odd, y_odd, x_first_ref, y_first_ref),
        (~x_odd, ~y_odd, x_second_ref, y_second_ref),
    ):
        x_start = pl.multiple_of(jnp.where(odd_x, 0, x_last), TILE)
        y_start = jnp.where(odd_y, 0, y_last)
        for field in range(FIELDS):
            x_ref[pl.ds(field * 96, 96), :] = prim_ref[pl.ds(field * CX * CY + x_start, 96), :]
            for layer in range(3):
                for block in range(2):
                    start = (field * CX + block * 8) * CY + layer
                    rows = pl.ds((field * 3 + layer) * CX + block * 8, 8)
                    y_ref[rows, :] = prim_ref[pl.ds(start + y_start, 8, stride=CY), :]


def unpack(*operands):
    grid_rows = jax.ShapeDtypeStruct((ROWS, CZ), jnp.float32)
    x_side = jax.ShapeDtypeStruct((FIELDS * 3 * CY, CZ), jnp.float32)
    y_side = jax.ShapeDtypeStruct((FIELDS * 3 * CX, CZ), jnp.float32)
    return call(
        unpack_kernel,
        "unpack",
        (grid_rows, grid_rows, x_side, x_side, y_side, y_side),
        [VMEM] * len(operands),
        scratch_shapes=[pltpu.VMEM((FIELDS, TILES, CELLS), jnp.float32)],
    )(*operands)


def median_zero(first_value, second_value):
    return jnp.maximum(
        jnp.minimum(first_value, 0.0), jnp.minimum(jnp.maximum(first_value, 0.0), second_value)
    )


def interface(prev, here, after, far):
    value = 7.0 / 12.0 * (here + after) - 1.0 / 12.0 * (prev + far)
    return jnp.minimum(jnp.maximum(value, jnp.minimum(here, after)), jnp.maximum(here, after))


def edges(centre, below, above):
    low, high = below - centre, above - centre
    return centre + median_zero(low, -2.0 * high), centre + median_zero(high, -2.0 * low)


def face_flux(left, right, normal):
    def speeds(side):
        scaled = 1.4 * side[4]
        sound = scaled * lax.rsqrt(scaled * side[0])
        return side[normal] - sound, side[normal] + sound

    left_low, left_high = speeds(left)
    right_low, right_high = speeds(right)
    slowest = jnp.minimum(jnp.minimum(left_low, right_low), 0.0)
    fastest = jnp.maximum(jnp.maximum(left_high, right_high), 0.0)
    inverse = 1.0 / (fastest - slowest)
    share_left = fastest * inverse
    share_right = -slowest * inverse
    spread = slowest * share_left
    rate_left = share_left * left[normal] - spread
    rate_right = share_right * right[normal] + spread
    mass_left, mass_right = rate_left * left[0], rate_right * right[0]
    push_left, push_right = share_left * left[4], share_right * right[4]
    flux = [mass_left + mass_right]
    for axis in range(1, 4):
        value = mass_left * left[axis] + mass_right * right[axis]
        if axis == normal:
            value = value + (push_left + push_right)
        flux.append(value)

    def carried(side, rate, mass, push):
        speed_square = side[1] * side[1] + side[2] * side[2] + side[3] * side[3]
        return 2.5 * (rate * side[4]) + 0.5 * (mass * speed_square) + push * side[normal]

    flux.append(
        carried(left, rate_left, mass_left, push_left) + carried(right, rate_right, mass_right, push_right)
    )
    return flux


def sweep(load, first, last, normal, emit):
    every = range(FIELDS)
    cells = {cell: load(cell) for cell in range(first - 3, first + 1)}
    below = [interface(*[cells[cell][f] for cell in range(first - 3, first + 1)]) for f in every]
    left = flux_below = None
    for cell in range(first - 1, last + 2):
        cells[cell + 2] = load(cell + 2)
        above = [
            interface(cells[cell - 1][f], cells[cell][f], cells[cell + 1][f], cells[cell + 2][f]) for f in every
        ]
        pairs = [edges(cells[cell][f], below[f], above[f]) for f in every]
        if left is not None:
            flux = face_flux(left, [pair[0] for pair in pairs], normal)
            if flux_below is not None:
                emit(cell - 1, [flux[f] - flux_below[f] for f in every])
            flux_below = flux
        left = [pair[1] for pair in pairs]
        below = above


def block_rows(f, cell, block):
    return pl.ds(pl.multiple_of((f * CX + cell) * CY + block * 8, 8), 8)


def inner_kernel(state_ref, prim_ref, out_ref):
    def rolled(value, shift):
        return pltpu.roll(value, shift % CZ, 1)

    ahead = (iota((CZ, CZ), 0) - iota((CZ, CZ), 1)) % CZ
    outer = jnp.where((ahead == CZ - 1) | (ahead == 2), -1.0, 0.0)
    weights = jnp.where(ahead <= 1, 7.0, outer).astype(jnp.bfloat16)
    lows, highs = [], []
    for f in range(FIELDS):
        value = prim_ref[pl.ds(f * CX * CY, CX * CY), :]
        after = rolled(value, -1)
        mean = weighted(value, weights) * (1.0 / 12.0)
        above = jnp.minimum(jnp.maximum(mean, jnp.minimum(value, after)), jnp.maximum(value, after))
        low, high = edges(value, rolled(above, 1), above)
        lows.append(rolled(low, -1))
        highs.append(high)
    flux = face_flux(highs, lows, 3)
    for f in range(FIELDS):
        rows = pl.ds(f * CX * CY, CX * CY)
        out_ref[rows, :] = state_ref[rows, :] - 0.1 * (flux[f] - rolled(flux[f], 1))

    def step(block, carry):
        def load(cell):
            return [prim_ref[block_rows(f, cell, block), :] for f in range(FIELDS)]

        def emit(cell, change):
            for f in range(FIELDS):
                rows = block_rows(f, cell, block)
                out_ref[rows, :] = out_ref[rows, :] - 0.1 * change[f]

        sweep(load, 3, CX - 4, 1, emit)
        return carry

    lax.fori_loop(0, CY // 8, step, 0)


def side(first_ref, second_ref, odd, before, rows):
    first, second = first_ref[rows, :], second_ref[rows, :]
    return jnp.where(odd, first, second) if before else jnp.where(odd, second, first)


def y_kernel(prim_ref, second_ref, first_ref, change_ref):
    odd = lax.axis_index("dev") % 2 == 1

    def step(block, carry):
        def load(cell):
            if cell < 0 or cell >= CY:
                layer = cell + 3 if cell < 0 else cell - CY
                rows = [pl.ds(pl.multiple_of((f * 3 + layer) * CX + block * 8, 8), 8) for f in range(FIELDS)]
                return [side(first_ref, second_ref, odd, cell < 0, row) for row in rows]
            return [prim_ref[pl.ds((f * CX + block * 8) * CY + cell, 8, stride=CY), :] for f in range(FIELDS)]

        def emit(cell, change):
            for f in range(FIELDS):
                rows = pl.ds(pl.multiple_of((f * CY + cell) * CX + block * 8, 8), 8)
                change_ref[rows, :] = change[f]

        sweep(load, 0, CY - 1, 2, emit)
        return carry

    lax.fori_loop(0, CX // 8, step, 0)


def x_kernel(before_ref, prim_ref, change_ref, first_ref, second_ref, out_hbm, out_ref, sems):
    odd = lax.axis_index("node") % 2 == 1

    def leaving(block, field):
        part = (field, slice(None), pl.ds(pl.multiple_of(block * 8, 8), 8))
        return pltpu.make_async_copy(out_ref.at[part], out_hbm.at[part], sems.at[block, field])

    def step(block, carry):
        def load(cell):
            if cell < 0 or cell >= CX:
                layer = cell + 3 if cell < 0 else cell - CX
                rows = [pl.ds(pl.multiple_of((f * 3 + layer) * CY + block * 8, 8), 8) for f in range(FIELDS)]
                return [side(first_ref, second_ref, odd, cell < 0, row) for row in rows]
            return [prim_ref[block_rows(f, cell, block), :] for f in range(FIELDS)]

        def emit(cell, change=None):
            for f in range(FIELDS):
                total = change_ref[pl.ds((f * CY + block * 8) * CX + cell, 8, stride=CX), :]
                if change is not None:
                    total = total + change[f]
                value = before_ref[block_rows(f, cell, block), :] - 0.1 * total
                out_ref[f, cell, pl.ds(pl.multiple_of(block * 8, 8), 8), :] = value

        sweep(load, 0, 2, 1, emit)
        for cell in range(3, CX - 3):
            emit(cell)
        sweep(load, CX - 3, CX - 1, 1, emit)
        for field in range(FIELDS):
            leaving(block, field).start()
        return carry

    lax.fori_loop(0, CY // 8, step, 0)
    for block in range(CY // 8):
        for field in range(FIELDS):
            leaving(block, field).wait()


def stage(kernel, name, *operands):
    return call(
        kernel,
        name,
        jax.ShapeDtypeStruct((ROWS, CZ), jnp.float32),
        [VMEM] * len(operands),
        cost_estimate=pl.CostEstimate(flops=20_000_000, bytes_accessed=4_000_000, transcendentals=200_000),
    )(*operands)


def finish(*operands):
    shape = (FIELDS, CX, CY, CZ)
    return pl.pallas_call(
        x_kernel,
        out_shape=jax.ShapeDtypeStruct(shape, jnp.float32),
        in_specs=[VMEM] * len(operands),
        out_specs=pl.BlockSpec(memory_space=pl.ANY),
        scratch_shapes=[pltpu.VMEM(shape, jnp.float32), pltpu.SemaphoreType.DMA((CY // 8, FIELDS))],
        compiler_params=pltpu.CompilerParams(vmem_limit_bytes=VMEM_LIMIT),
        name="flux_first",
    )(*operands)


def shifted(value, axes, count, target):
    pairs = [(i, target(i)) for i in range(count)]
    return lax.ppermute(value, axes, [pair for pair in pairs if pair[1] >= 0])


def hop(device, step):
    return device + 8 * step if 0 <= device // 8 + step < 16 else -1


def next_node(device):
    other = hop(device, 1 if device % 8 >= 4 else -1)
    return other if other >= 0 else device ^ 6


def onward_node(device):
    dev = device % 8
    return device if 2 <= dev < 6 else hop(device, 1 if dev < 2 else -1)


def masked(value, mask):
    return shifted(value, AXES, 128, lambda device: device ^ mask)


def body(old_state, old_tile_pos):
    pos = old_tile_pos.reshape(1, TILES)
    old = old_state.transpose(1, 0, 2)
    two, three, six, seven, relay = pack_early(pos, old)
    relay = shifted(relay, AXES, 128, next_node)
    six, seven, two, three = masked(six, 6), masked(seven, 7), masked(two, 2), masked(three, 3)
    one, four, five, far, onward = pack_late(pos, old, relay, six, seven)
    onward = shifted(onward, AXES, 128, onward_node)
    four, five, one, far = masked(four, 4), masked(five, 5), masked(one, 1), masked(far, 64)
    state, prim, x_first, x_second, y_first, y_second = unpack(
        pos, old, one, two, three, four, five, far, onward
    )
    x_first = shifted(x_first, "node", 16, lambda i: i ^ 1)
    x_second = shifted(x_second, "node", 16, lambda i: (i + 1) % 16 if i % 2 else (i - 1) % 16)
    y_first = shifted(y_first, "dev", 8, lambda i: i ^ 1)
    y_second = shifted(y_second, "dev", 8, lambda i: (i + 1) % 8 if i % 2 else (i - 1) % 8)
    result = stage(inner_kernel, "flux_inner", state, prim)
    change = stage(y_kernel, "flux_second", prim, y_second, y_first)
    return finish(result, prim, change, x_first, x_second)


def solution(mesh):
    in_specs = (P(AXES, None, None), P(AXES))
    out_specs = P(None, "node", "dev", None)
    return jax.shard_map(body, mesh=mesh, in_specs=in_specs, out_specs=out_specs, check_vma=False)
```

```python
import jax
import jax.numpy as jnp
from jax import lax
from jax.experimental import pallas as pl
from jax.experimental.pallas import tpu as pltpu
from jax.sharding import PartitionSpec as P

CX = 16
CY = 32
CZ = 128
FIELDS = 5
TILE = 8
MOVE = 8
TILES = 128
CELLS = 512
PARTS = CELLS // CZ
PLANES = FIELDS * PARTS + 1
ROWS = FIELDS * CX * CY
VMEM_LIMIT = 48 * 1024 * 1024

EARLY_RELAY = 4 * MOVE
EARLY_ROWS = 6 * MOVE
LATE_ROWS = 4 * MOVE
ARRIVED = 9 * MOVE

AXES = ("node", "dev")


def iota(shape, dim):
    return lax.broadcasted_iota(jnp.int32, shape, dim)


def split3(value):
    high = value.astype(jnp.bfloat16)
    rest = value - high.astype(jnp.float32)
    mid = rest.astype(jnp.bfloat16)
    low = (rest - mid.astype(jnp.float32)).astype(jnp.bfloat16)
    return high, mid, low


def added(terms):
    total = None
    for term in terms:
        total = term if total is None else total + term
    return total


def pick(choice, values):
    return added(
        jnp.dot(choice, part, preferred_element_type=jnp.float32) for part in reversed(split3(values))
    )


def weighted(values, weights):
    return added(
        jnp.dot(part, weights, preferred_element_type=jnp.float32) for part in reversed(split3(values))
    )


def place():
    return lax.axis_index("node"), lax.axis_index("dev")


def targets(pos):
    square = (TILES, TILES)
    by_lane = jnp.broadcast_to(pos // TILES, square)
    by_row = by_lane.T
    earlier = (by_lane == by_row) & (iota(square, 0) < iota(square, 1))
    rank = jnp.sum(earlier.astype(jnp.int32), axis=0, keepdims=True)
    return pos // TILES, pos % TILES, rank


def packed(target, local, rows, old_ref, put):
    shape = (rows, TILES)
    chosen = iota(shape, 0) == jnp.broadcast_to(target, shape)
    code = jnp.sum(
        jnp.where(chosen, jnp.broadcast_to(local + 1, shape), 0).astype(jnp.float32), axis=1, keepdims=True
    )
    put(PLANES - 1, jnp.broadcast_to(code, shape))
    choice = chosen.astype(jnp.float32).astype(jnp.bfloat16)
    for field in range(FIELDS):
        values = pick(choice, old_ref[field])
        for part in range(PARTS):
            put(field * PARTS + part, values[:, part * CZ : (part + 1) * CZ])


def pack_early_kernel(pos_ref, old_ref, two_ref, three_ref, six_ref, seven_ref, relay_ref):
    node, dev = place()
    owner, local, rank = targets(pos_ref[...])
    mask = (owner % 8) ^ dev
    outer, low = mask >= 4, mask % 4
    here = owner // 8 == node
    by_mask = (mask // 4 * 2 + mask % 2) * MOVE + rank
    relayed = EARLY_RELAY + mask % 2 * MOVE + rank
    target = jnp.where(low >= 2, by_mask, jnp.where(outer & ~here, relayed, -1))
    target = jnp.where(owner // 8 == node ^ 8, -1, target)

    def put(plane, value):
        for block, ref in enumerate((two_ref, three_ref, six_ref, seven_ref)):
            ref[plane] = value[block * MOVE : (block + 1) * MOVE]
        for block in range(2):
            first = EARLY_RELAY + block * MOVE
            relay_ref[block, plane] = value[first : first + MOVE]

    packed(target, local, EARLY_ROWS, old_ref, put)


def pack_late_kernel(
    pos_ref, old_ref, relay_ref, six_ref, seven_ref, one_ref, four_ref, five_ref, far_ref, on_ref
):
    node, dev = place()
    owner, local, rank = targets(pos_ref[...])
    mask = (owner % 8) ^ dev
    inside = jnp.where((mask == 1) | (mask == 4) | (mask == 5), (mask // 4 + mask % 2) * MOVE, -TILES)
    inside = jnp.where(mask == 1, 0, inside)
    target = jnp.where(owner // 8 == node, inside, jnp.where(owner // 8 == node ^ 8, 3 * MOVE, -TILES)) + rank

    def put(plane, value):
        one_ref[plane] = value[:MOVE]
        four_ref[0, plane] = value[MOVE : 2 * MOVE]
        four_ref[1, plane] = relay_ref[0, plane]
        five_ref[plane] = value[2 * MOVE : 3 * MOVE] + relay_ref[1, plane]
        far_ref[plane] = value[3 * MOVE :]
        on_ref[0, plane] = six_ref[plane]
        on_ref[1, plane] = seven_ref[plane]

    packed(target, local, LATE_ROWS, old_ref, put)


VMEM = pl.BlockSpec(memory_space=pltpu.VMEM)
BUFFER = jax.ShapeDtypeStruct((PLANES, MOVE, CZ), jnp.float32)


def buffers(count):
    return jax.ShapeDtypeStruct((count,) + BUFFER.shape, jnp.float32)


def call(kernel, name, out_shape, in_specs, **more):
    return pl.pallas_call(
        kernel,
        out_shape=out_shape,
        in_specs=in_specs,
        out_specs=jax.tree.map(lambda _: VMEM, out_shape),
        compiler_params=pltpu.CompilerParams(vmem_limit_bytes=VMEM_LIMIT),
        name=name,
        **more,
    )


def pack_early(pos, old):
    return call(pack_early_kernel, "pack_early", (BUFFER,) * 4 + (buffers(2),), [VMEM, VMEM])(pos, old)


def pack_late(pos, old, relay, six, seven):
    return call(
        pack_late_kernel, "pack_late", (BUFFER, buffers(2), BUFFER, BUFFER, buffers(2)), [VMEM] * 5
    )(pos, old, relay, six, seven)


def grains(first, second, half_low, row_pick, lane_picks):
    first = pltpu.roll(first, 0, 1, stride=TILE, stride_axis=0)
    second = pltpu.roll(second, 64, 1, stride=TILE, stride_axis=0)
    result = []
    for half in range(2):
        mixed = jnp.where(half_low, first, second) if half == 0 else jnp.where(half_low, second, first)
        mixed = jnp.take_along_axis(mixed, row_pick, axis=0)
        result.append(jnp.take_along_axis(mixed, lane_picks[half], axis=1))
    return result


def unpack_kernel(
    pos_ref, old_ref, one_ref, two_ref, three_ref, four_ref, five_ref, far_ref, on_ref,
    state_ref, prim_ref, x_first_ref, x_second_ref, y_first_ref, y_second_ref, tiles_ref,
):
    node, dev = place()
    pos = pos_ref[...]
    square = (TILES, TILES)
    kept = jnp.where(pos // TILES == node * 8 + dev, pos % TILES, -1)
    kept_choice = jnp.broadcast_to(kept, square) == iota(square, 0)

    def arrived(plane):
        blocks = [ref[plane] for ref in (one_ref, two_ref, three_ref, five_ref, far_ref)]
        blocks += [four_ref[0, plane], four_ref[1, plane]]
        blocks += [on_ref[0, plane], on_ref[1, plane]]
        return jnp.concatenate(blocks, axis=0)

    code = jnp.concatenate([arrived(PLANES - 1), jnp.zeros((TILES - ARRIVED, CZ), jnp.float32)], axis=0)
    code = code.T.astype(jnp.int32)
    new_choice = code == iota(square, 0) + 1
    choice = jnp.concatenate([kept_choice, new_choice], axis=1).astype(jnp.float32).astype(jnp.bfloat16)
    blank = jnp.zeros((TILES - ARRIVED, CELLS), jnp.float32)
    for field in range(FIELDS):
        moved = jnp.concatenate([arrived(field * PARTS + part) for part in range(PARTS)], axis=1)
        tiles_ref[field] = pick(choice, jnp.concatenate([old_ref[field], moved, blank], axis=0))

    row = iota((TILE, CZ), 0)
    grain = iota((TILE, CZ), 1) // TILE
    half_low = (grain - row) % 16 < 8
    row_pick = (grain - row) % 8
    lane = iota((TILE, CZ), 1)
    lane_picks = [(lane + TILE * row + 64 * half) % CZ for half in range(2)]

    def brick(index, carry):
        across, up = index // 4, index % 4
        for part in range(PARTS):
            blocks = []
            for field in range(FIELDS):
                lanes = slice(part * CZ, (part + 1) * CZ)
                first = tiles_ref[field, pl.ds(pl.multiple_of(index * 16, 16), 8), lanes]
                second = tiles_ref[field, pl.ds(pl.multiple_of(index * 16 + 8, 8), 8), lanes]
                blocks.append(grains(first, second, half_low, row_pick, lane_picks))
            for half in range(2):
                density, mom_x, mom_y, mom_z, energy = [blocks[field][half] for field in range(FIELDS)]
                inverse = 1.0 / density
                vel = [mom_x * inverse, mom_y * inverse, mom_z * inverse]
                square_sum = vel[0] * vel[0] + vel[1] * vel[1] + vel[2] * vel[2]
                pressure = (1.4 - 1.0) * (energy - 0.5 * density * square_sum)
                cell_x = across * TILE + part * 2 + half
                for field in range(FIELDS):
                    start = pl.multiple_of((field * CX + cell_x) * CY + up * TILE, TILE)
                    state_ref[pl.ds(start, TILE), :] = blocks[field][half]
                    prim_ref[pl.ds(start, TILE), :] = density if field == 0 else (
                        pressure if field == 4 else vel[field - 1]
                    )
        return carry

    lax.fori_loop(0, 8, brick, 0)
    x_odd, y_odd = node % 2 == 1, dev % 2 == 1
    x_last, y_last = (CX - 3) * CY, CY - 3
    for odd_x, odd_y, x_ref, y_ref in (
        (x_odd, y_odd, x_first_ref, y_first_ref),
        (~x_odd, ~y_odd, x_second_ref, y_second_ref),
    ):
        x_start = pl.multiple_of(jnp.where(odd_x, 0, x_last), TILE)
        y_start = jnp.where(odd_y, 0, y_last)
        for field in range(FIELDS):
            x_ref[pl.ds(field * 96, 96), :] = prim_ref[pl.ds(field * CX * CY + x_start, 96), :]
            for layer in range(3):
                for block in range(2):
                    start = (field * CX + block * 8) * CY + layer
                    rows = pl.ds((field * 3 + layer) * CX + block * 8, 8)
                    y_ref[rows, :] = prim_ref[pl.ds(start + y_start, 8, stride=CY), :]


def unpack(*operands):
    grid_rows = jax.ShapeDtypeStruct((ROWS, CZ), jnp.float32)
    x_side = jax.ShapeDtypeStruct((FIELDS * 3 * CY, CZ), jnp.float32)
    y_side = jax.ShapeDtypeStruct((FIELDS * 3 * CX, CZ), jnp.float32)
    return call(
        unpack_kernel,
        "unpack",
        (grid_rows, grid_rows, x_side, x_side, y_side, y_side),
        [VMEM] * len(operands),
        scratch_shapes=[pltpu.VMEM((FIELDS, TILES, CELLS), jnp.float32)],
    )(*operands)


def median_zero(first_value, second_value):
    return jnp.maximum(
        jnp.minimum(first_value, 0.0), jnp.minimum(jnp.maximum(first_value, 0.0), second_value)
    )


def interface(prev, here, after, far):
    value = 7.0 / 12.0 * (here + after) - 1.0 / 12.0 * (prev + far)
    return jnp.minimum(jnp.maximum(value, jnp.minimum(here, after)), jnp.maximum(here, after))


def edges(centre, below, above):
    low, high = below - centre, above - centre
    return centre + median_zero(low, -2.0 * high), centre + median_zero(high, -2.0 * low)


def face_flux(left, right, normal):
    def speeds(side):
        scaled = 1.4 * side[4]
        sound = scaled * lax.rsqrt(scaled * side[0])
        return side[normal] - sound, side[normal] + sound

    left_low, left_high = speeds(left)
    right_low, right_high = speeds(right)
    slowest = jnp.minimum(jnp.minimum(left_low, right_low), 0.0)
    fastest = jnp.maximum(jnp.maximum(left_high, right_high), 0.0)
    inverse = 1.0 / (fastest - slowest)
    share_left = fastest * inverse
    share_right = -slowest * inverse
    spread = slowest * share_left
    rate_left = share_left * left[normal] - spread
    rate_right = share_right * right[normal] + spread
    mass_left, mass_right = rate_left * left[0], rate_right * right[0]
    push_left, push_right = share_left * left[4], share_right * right[4]
    flux = [mass_left + mass_right]
    for axis in range(1, 4):
        value = mass_left * left[axis] + mass_right * right[axis]
        if axis == normal:
            value = value + (push_left + push_right)
        flux.append(value)

    def carried(side, rate, mass, push):
        speed_square = side[1] * side[1] + side[2] * side[2] + side[3] * side[3]
        return 2.5 * (rate * side[4]) + 0.5 * (mass * speed_square) + push * side[normal]

    flux.append(
        carried(left, rate_left, mass_left, push_left) + carried(right, rate_right, mass_right, push_right)
    )
    return flux


def sweep(load, first, last, normal, emit):
    every = range(FIELDS)
    cells = {cell: load(cell) for cell in range(first - 3, first + 1)}
    below = [interface(*[cells[cell][f] for cell in range(first - 3, first + 1)]) for f in every]
    left = flux_below = None
    for cell in range(first - 1, last + 2):
        cells[cell + 2] = load(cell + 2)
        above = [
            interface(cells[cell - 1][f], cells[cell][f], cells[cell + 1][f], cells[cell + 2][f]) for f in every
        ]
        pairs = [edges(cells[cell][f], below[f], above[f]) for f in every]
        if left is not None:
            flux = face_flux(left, [pair[0] for pair in pairs], normal)
            if flux_below is not None:
                emit(cell - 1, [flux[f] - flux_below[f] for f in every])
            flux_below = flux
        left = [pair[1] for pair in pairs]
        below = above


def block_rows(f, cell, block):
    return pl.ds(pl.multiple_of((f * CX + cell) * CY + block * 8, 8), 8)


def inner_kernel(state_ref, prim_ref, out_ref):
    def rolled(value, shift):
        return pltpu.roll(value, shift % CZ, 1)

    ahead = (iota((CZ, CZ), 0) - iota((CZ, CZ), 1)) % CZ
    outer = jnp.where((ahead == CZ - 1) | (ahead == 2), -1.0, 0.0)
    weights = jnp.where(ahead <= 1, 7.0, outer).astype(jnp.bfloat16)
    lows, highs = [], []
    for f in range(FIELDS):
        value = prim_ref[pl.ds(f * CX * CY, CX * CY), :]
        after = rolled(value, -1)
        mean = weighted(value, weights) * (1.0 / 12.0)
        above = jnp.minimum(jnp.maximum(mean, jnp.minimum(value, after)), jnp.maximum(value, after))
        low, high = edges(value, rolled(above, 1), above)
        lows.append(rolled(low, -1))
        highs.append(high)
    flux = face_flux(highs, lows, 3)
    for f in range(FIELDS):
        rows = pl.ds(f * CX * CY, CX * CY)
        out_ref[rows, :] = state_ref[rows, :] - 0.1 * (flux[f] - rolled(flux[f], 1))

    def step(block, carry):
        def load(cell):
            return [prim_ref[block_rows(f, cell, block), :] for f in range(FIELDS)]

        def emit(cell, change):
            for f in range(FIELDS):
                rows = block_rows(f, cell, block)
                out_ref[rows, :] = out_ref[rows, :] - 0.1 * change[f]

        sweep(load, 3, CX - 4, 1, emit)
        return carry

    lax.fori_loop(0, CY // 8, step, 0)


def side(first_ref, second_ref, odd, before, rows):
    first, second = first_ref[rows, :], second_ref[rows, :]
    return jnp.where(odd, first, second) if before else jnp.where(odd, second, first)


def y_kernel(prim_ref, second_ref, first_ref, change_ref):
    odd = lax.axis_index("dev") % 2 == 1

    def step(block, carry):
        def load(cell):
            if cell < 0 or cell >= CY:
                layer = cell + 3 if cell < 0 else cell - CY
                rows = [pl.ds(pl.multiple_of((f * 3 + layer) * CX + block * 8, 8), 8) for f in range(FIELDS)]
                return [side(first_ref, second_ref, odd, cell < 0, row) for row in rows]
            return [prim_ref[pl.ds((f * CX + block * 8) * CY + cell, 8, stride=CY), :] for f in range(FIELDS)]

        def emit(cell, change):
            for f in range(FIELDS):
                rows = pl.ds(pl.multiple_of((f * CY + cell) * CX + block * 8, 8), 8)
                change_ref[rows, :] = change[f]

        sweep(load, 0, CY - 1, 2, emit)
        return carry

    lax.fori_loop(0, CX // 8, step, 0)


def x_kernel(before_ref, prim_ref, change_ref, first_ref, second_ref, out_hbm, out_ref, sems):
    odd = lax.axis_index("node") % 2 == 1

    spans = ((3, CX - 6), (0, 3), (CX - 3, 3))

    def leaving(block, field, span):
        first, count = spans[span]
        part = (field, pl.ds(first, count), pl.ds(pl.multiple_of(block * 8, 8), 8))
        return pltpu.make_async_copy(out_ref.at[part], out_hbm.at[part], sems.at[block, field, span])

    def step(block, carry):
        def load(cell):
            if cell < 0 or cell >= CX:
                layer = cell + 3 if cell < 0 else cell - CX
                rows = [pl.ds(pl.multiple_of((f * 3 + layer) * CY + block * 8, 8), 8) for f in range(FIELDS)]
                return [side(first_ref, second_ref, odd, cell < 0, row) for row in rows]
            return [prim_ref[block_rows(f, cell, block), :] for f in range(FIELDS)]

        def emit(cell, change=None):
            for f in range(FIELDS):
                total = change_ref[pl.ds((f * CY + block * 8) * CX + cell, 8, stride=CX), :]
                if change is not None:
                    total = total + change[f]
                value = before_ref[block_rows(f, cell, block), :] - 0.1 * total
                out_ref[f, cell, pl.ds(pl.multiple_of(block * 8, 8), 8), :] = value

        for cell in range(3, CX - 3):
            emit(cell)
        for field in range(FIELDS):
            leaving(block, field, 0).start()
        sweep(load, 0, 2, 1, emit)
        sweep(load, CX - 3, CX - 1, 1, emit)
        for field in range(FIELDS):
            leaving(block, field, 1).start()
            leaving(block, field, 2).start()
        return carry

    lax.fori_loop(0, CY // 8, step, 0)
    for block in range(CY // 8):
        for field in range(FIELDS):
            for span in range(3):
                leaving(block, field, span).wait()


def stage(kernel, name, *operands):
    return call(
        kernel,
        name,
        jax.ShapeDtypeStruct((ROWS, CZ), jnp.float32),
        [VMEM] * len(operands),
        cost_estimate=pl.CostEstimate(flops=20_000_000, bytes_accessed=4_000_000, transcendentals=200_000),
    )(*operands)


def finish(*operands):
    shape = (FIELDS, CX, CY, CZ)
    return pl.pallas_call(
        x_kernel,
        out_shape=jax.ShapeDtypeStruct(shape, jnp.float32),
        in_specs=[VMEM] * len(operands),
        out_specs=pl.BlockSpec(memory_space=pl.ANY),
        scratch_shapes=[pltpu.VMEM(shape, jnp.float32), pltpu.SemaphoreType.DMA((CY // 8, FIELDS, 3))],
        compiler_params=pltpu.CompilerParams(vmem_limit_bytes=VMEM_LIMIT),
        name="flux_first",
    )(*operands)


def shifted(value, axes, count, target):
    pairs = [(i, target(i)) for i in range(count)]
    return lax.ppermute(value, axes, [pair for pair in pairs if pair[1] >= 0])


def hop(device, step):
    return device + 8 * step if 0 <= device // 8 + step < 16 else -1


def next_node(device):
    other = hop(device, 1 if device % 8 >= 4 else -1)
    return other if other >= 0 else device ^ 6


def onward_node(device):
    dev = device % 8
    return device if 2 <= dev < 6 else hop(device, 1 if dev < 2 else -1)


def masked(value, mask):
    return shifted(value, AXES, 128, lambda device: device ^ mask)


def body(old_state, old_tile_pos):
    pos = old_tile_pos.reshape(1, TILES)
    old = old_state.transpose(1, 0, 2)
    two, three, six, seven, relay = pack_early(pos, old)
    relay = shifted(relay, AXES, 128, next_node)
    six, seven, two, three = masked(six, 6), masked(seven, 7), masked(two, 2), masked(three, 3)
    one, four, five, far, onward = pack_late(pos, old, relay, six, seven)
    onward = shifted(onward, AXES, 128, onward_node)
    four, five, one, far = masked(four, 4), masked(five, 5), masked(one, 1), masked(far, 64)
    state, prim, x_first, x_second, y_first, y_second = unpack(
        pos, old, one, two, three, four, five, far, onward
    )
    x_first = shifted(x_first, "node", 16, lambda i: i ^ 1)
    x_second = shifted(x_second, "node", 16, lambda i: (i + 1) % 16 if i % 2 else (i - 1) % 16)
    y_first = shifted(y_first, "dev", 8, lambda i: i ^ 1)
    y_second = shifted(y_second, "dev", 8, lambda i: (i + 1) % 8 if i % 2 else (i - 1) % 8)
    result = stage(inner_kernel, "flux_inner", state, prim)
    change = stage(y_kernel, "flux_second", prim, y_second, y_first)
    return finish(result, prim, change, x_first, x_second)


def solution(mesh):
    in_specs = (P(AXES, None, None), P(AXES))
    out_specs = P(None, "node", "dev", None)
    return jax.shard_map(body, mesh=mesh, in_specs=in_specs, out_specs=out_specs, check_vma=False)
```
